256 devices in a mesh: seq: 128 (over y, x, z), head: 2 (over core).
Axes of the slice: x: 4, y: 4, z: 8, core: 2. Of those that a mesh axis runs over, the one named last changes fastest.
Arguments:
- query_raw: bfloat16 [16384, 2048], P('seq', 'head'), may hold values from -6 to 6
- key_raw: bfloat16 [16384, 2048], P('seq', 'head'), may hold values from -6 to 6
- value_raw: bfloat16 [16384, 2048], P('seq', 'head'), may hold values from -6 to 6
- gate_raw: float32 [16384, 2048], P('seq', 'head')
- beta_raw: float32 [16384, 16], P('seq', 'head'), may hold values from -8.5 to 3.5
- conv_weight: float32 [3, 4, 2048], P(None, None, 'head'), may hold values from -3 to 3
- decay_log: float32 [2048], P('head')
- grad_out: bfloat16 [16384, 2048], P('seq', 'head'), may hold values from -6 to 6
Outputs:
- query_grad: bfloat16 [16384, 2048], P('seq', 'head')
- key_grad: bfloat16 [16384, 2048], P('seq', 'head')
- value_grad: bfloat16 [16384, 2048], P('seq', 'head')
- gate_grad: float32 [16384, 2048], P('seq', 'head')
- beta_grad: float32 [16384, 16], P('seq', 'head')
- conv_grad: float32 [3, 4, 2048], P(None, None, 'head')
- decay_grad: float32 [2048], P('head')
The draws below stay inside these ranges and needn't reach their ends.
All inputs are finite; a program needn't handle non-finite values.
Results may differ from the reference program's by a relative error of at most 0.0018.
Values may be sent and summed in bfloat16 or wider, within the bound.
No kernel may reach another device: no remote copies, remote signals or barrier semaphores. Data moves between devices by JAX's collectives and lax.ppermute only.
A program may use at most 128 MiB of HBM per device.

```python
import jax
import jax.numpy as jnp
from jax import lax

HEADS = 16
DK = 128
KCONV = 4
TOK_DEV = 128
TOKENS = 16384
CH = 2048


def gate_parts(key):
    base = jax.random.fold_in(key, 7)
    pick_key, fast_key, slow_key, normal_key, spot_key, loss_key = jax.random.split(base, 6)
    channels = HEADS * DK
    share = 0.5
    slow = jax.random.uniform(pick_key, (channels,)) < share
    fast_speed = jnp.exp(jax.random.uniform(fast_key, (channels,), minval=jnp.log(1.0 / 50.0), maxval=jnp.log(1.0 / 30.0)))
    slow_speed = jnp.log(10.0) / TOKENS * jnp.exp(jax.random.uniform(slow_key, (channels,), minval=jnp.log(0.02), maxval=jnp.log(0.2)))
    speed = jnp.where(slow, slow_speed, fast_speed)
    decay_values = jnp.log(speed / 0.8)
    score_logits = jnp.clip(jax.random.normal(normal_key, (TOKENS, channels)), -3.0, 3.0)
    spots = jax.random.randint(spot_key, (3,), 0, TOKENS)
    losses = jax.random.uniform(loss_key, (channels,), minval=0.22, maxval=0.5)
    target_value = losses / (speed / 0.8)
    spike_amount = target_value + jnp.log(-jnp.expm1(-target_value))
    positions = jnp.arange(TOKENS)
    flagged_entries = jnp.any(positions[:, None] == spots[None, :], axis=1)
    score_logits = jnp.where(flagged_entries[:, None], spike_amount[None, :], score_logits)
    return (decay_values.astype(jnp.float32), score_logits.astype(jnp.float32))


def draw_decay_log(key, part):
    return gate_parts(key)[0]


def draw_gate_raw(key, part):
    return gate_parts(key)[1]


def draw_beta_raw(key, part):
    center_key, noise_key = jax.random.split(jax.random.fold_in(key, 3))
    centers = jax.random.uniform(center_key, (HEADS,), minval=-6.0, maxval=1.0)
    noise = jnp.clip(jax.random.normal(noise_key, (TOKENS, HEADS)), -2.5, 2.5) * 0.8
    return (centers[None, :] + noise).astype(jnp.float32)


def block_scale(rng, dims, cuts, low, largest):
    def one(axis_at, parts):
        heights = jax.random.uniform(jax.random.fold_in(jax.random.fold_in(rng, 6), axis_at), (parts,), jnp.float32, low / len(cuts), largest / len(cuts))
        return jnp.repeat(jnp.exp(heights), dims[axis_at] // parts).reshape((-1,) + (1,) * (len(dims) - axis_at - 1))

    loudness = one(*cuts[0])
    for cut in cuts[1:]:
        loudness = loudness * one(*cut)
    return loudness


def centred(rng, dims, deviation, limit, shards=(), held_as=jnp.bfloat16):
    result = jax.random.normal(rng, dims, jnp.float32) * deviation
    if len(shards) > 0:
        result = block_scale(rng, dims, shards, -0.22, 0.18) * result
    return jnp.clip(result, min=-limit, max=limit).astype(held_as)


def setup_inputs(seed: int = 0) -> dict:
    arg_keys = jax.random.split(jax.random.key(seed), 9)
    return {
        "query_raw": centred(arg_keys[0], (TOKENS, CH), 1.0, 6.0, ((0, 128), (1, 2))),
        "key_raw": centred(arg_keys[1], (TOKENS, CH), 1.0, 6.0, ((0, 128), (1, 2))),
        "value_raw": centred(arg_keys[2], (TOKENS, CH), 1.0, 6.0, ((0, 128), (1, 2))),
        "gate_raw": draw_gate_raw(jax.random.fold_in(arg_keys[8], 71), 0),
        "beta_raw": draw_beta_raw(jax.random.fold_in(arg_keys[8], 71), 0),
        "conv_weight": centred(arg_keys[5], (3, KCONV, CH), KCONV ** -0.5, 3.0, ((2, 2),), jnp.float32),
        "decay_log": draw_decay_log(jax.random.fold_in(arg_keys[8], 71), 0),
        "grad_out": centred(arg_keys[7], (TOKENS, CH), 1.0, 6.0, ((0, 128), (1, 2))),
    }


largest_entry = lax.Precision.HIGHEST
epsilon = 1e-06

def conv_silu(source, weights):
    margin = weights.shape[0] - 1
    length = source.shape[0]
    padded = jnp.concatenate([jnp.zeros((margin, source.shape[1]), jnp.float32), source], 0)
    summed = weights[0] * padded[0:length]
    for offset in range(1, weights.shape[0]):
        summed = summed + weights[offset] * padded[offset:offset + length]
    return jax.nn.silu(summed)

def unit_heads(vectors):
    return vectors * lax.rsqrt(lax.optimization_barrier(jnp.sum(vectors * vectors, axis=-1, keepdims=True)) + epsilon)

def layer_outputs(query_in, key_in, value_in, gate_in, beta_in, conv_in, decay_in):
    length = gate_in.shape[0]
    head_count = beta_in.shape[1]
    head_width = gate_in.shape[1] // head_count
    head_shape = (length, head_count, head_width)
    queries = unit_heads(conv_silu(query_in, conv_in[0]).reshape(head_shape))
    keys = unit_heads(conv_silu(key_in, conv_in[1]).reshape(head_shape))
    values = conv_silu(value_in, conv_in[2]).reshape(head_shape)
    log_decay = (-jnp.exp(decay_in) * jax.nn.softplus(gate_in)).reshape(head_shape)
    beta_rate = jax.nn.sigmoid(beta_in)
    block_count = length // TOK_DEV

    def token_step(recall_memory, sliced):
        single_query_row, single_key_row, value_row, decay_row, beta_row = sliced
        recall_memory = recall_memory * jnp.exp(decay_row)[:, :, None]
        predicted_value = jnp.einsum('pjf,pj->pf', recall_memory, single_key_row, precision=largest_entry)
        recall_memory = recall_memory + beta_row[:, None, None] * single_key_row[:, :, None] * (value_row - predicted_value)[:, None, :]
        return (recall_memory, jnp.einsum('pjf,pj->pf', recall_memory, single_query_row, precision=largest_entry))

    def block_step(recall_memory, sliced):
        return lax.scan(token_step, recall_memory, sliced)
    blocked = tuple((array.reshape((block_count, TOK_DEV) + array.shape[1:]) for array in (queries, keys, values, log_decay, beta_rate)))
    initial = jnp.zeros((head_count, head_width, head_width), jnp.float32)
    unused, outputs = lax.scan(jax.checkpoint(block_step), initial, blocked)
    return outputs.reshape(length, head_count * head_width)

def reference(query_raw, key_raw, value_raw, gate_raw, beta_raw, conv_weight, decay_log, grad_out):
    primal, pullback = jax.vjp(layer_outputs, query_raw.astype(jnp.float32), key_raw.astype(jnp.float32), value_raw.astype(jnp.float32), gate_raw, beta_raw, conv_weight, decay_log)
    grads = pullback(grad_out.astype(jnp.float32))
    return (grads[0].astype(jnp.bfloat16), grads[1].astype(jnp.bfloat16), grads[2].astype(jnp.bfloat16), grads[3], grads[4], grads[5], grads[6])
```

```python
import functools

import jax
import jax.numpy as jnp
from jax import lax
from jax.experimental import pallas as pl
from jax.experimental.pallas import tpu as pltpu
from jax.sharding import Mesh
from jax.sharding import PartitionSpec as P

F32 = jnp.float32
BF16 = jnp.bfloat16
EPS = 1e-06
T = 128
SEQ = ("y", "x", "z")
NN = (((1,), (0,)), ((), ()))
NT = (((1,), (1,)), ((), ()))
TN = (((0,), (0,)), ((), ()))
MIB = 1024 * 1024


def split(x):
    hi = x.astype(BF16)
    return (hi, (x - hi.astype(F32)).astype(BF16))


def dot(a, b, dims):
    total = None
    for i, left in enumerate(a):
        for j, right in enumerate(b):
            if i + j < 2:
                term = lax.dot_general(left, right, dims, preferred_element_type=F32)
                total = term if total is None else total + term
    return total


def lanes(*parts):
    return tuple(jnp.concatenate(terms, axis=1) for terms in zip(*parts))


def rows(*parts):
    return tuple(jnp.concatenate(terms, axis=0) for terms in zip(*parts))


def iota(shape, dim):
    return lax.broadcasted_iota(jnp.int32, shape, dim)


def sigmoid(x):
    return 1.0 / (1.0 + jnp.exp(-x))


def column(block, head):
    return jnp.sum(jnp.where(iota(block.shape, 1) == head, block, 0.0), axis=1, keepdims=True)


def gate_factors(cumul):
    row = iota((T, T), 0)
    late = row >= T // 2
    mid0 = cumul[T // 4 : T // 4 + 1]
    mid1 = cumul[3 * T // 4 : 3 * T // 4 + 1]
    last = cumul[T - 1 : T]
    up0 = jnp.exp(cumul - mid0)
    up1 = jnp.where(late, jnp.exp(jnp.where(late, cumul - mid1, 0.0)), 0.0)
    down = jnp.exp(jnp.where(late, mid1, mid0) - cumul)
    return up0, up1, down, jnp.exp(cumul), jnp.exp(last - cumul), jnp.exp(last), late


def unit_inverse(coupling):
    row, col = iota((T, T), 0), iota((T, T), 1)
    ident = jnp.where(row == col, 1.0, 0.0)

    def same(size):
        return (row // size) == (col // size)

    inner = [jnp.where(same(16), c, 0.0) for c in coupling]
    result = [ident - c for c in inner]
    power = []
    for c in inner:
        s = split(c)
        power.append(dot(s, s, NN))
    for level in range(2):
        out = []
        for p, r in zip(power, result):
            s = split(p)
            out.append(dot(rows(s, split(r)), s, NN))
        power = [o[:T] for o in out]
        result = [r + o[T:] for r, o in zip(result, out)]
    result = [r + dot(split(r), split(p), NN) for r, p in zip(result, power)]
    for size in (32, 64, 128):
        pick = same(size) & ~same(size // 2)
        parts = [split(r) for r in result]
        half = [dot(split(jnp.where(pick, c, 0.0)), s, NN) for c, s in zip(coupling, parts)]
        result = [r - dot(s, split(h), NN) for r, s, h in zip(result, parts, half)]
    return result


def maps_kernel(
    heads,
    q_ref, k_ref, v_ref, halo_ref, gate_ref, beta_ref, conv_ref, decay_ref, grad_ref,
    maps_ref, q_out, k_out, fq_out, fk_out, fv_out, cum_out, gf_out, ld_out, w_out, u_out, pg_out, inv_out,
    ext,
):
    row, col = iota((T, T), 0), iota((T, T), 1)
    strict = row > col
    lower = row >= col
    ident = jnp.where(row == col, 1.0, 0.0)
    tri = jnp.where(lower, 1.0, 0.0).astype(BF16)
    beta_all = sigmoid(beta_ref[...])
    base = pl.program_id(0) * heads
    each = range(heads)
    at = [slice(h * T, (h + 1) * T) for h in each]
    cumul, qs, ks, vs, betas = [], [], [], [], []
    for h in each:
        gate = gate_ref[:, at[h]]
        speed = -jnp.exp(decay_ref[:, at[h]])
        log_decay = speed * (jnp.maximum(gate, 0.0) + jnp.log1p(jnp.exp(-jnp.abs(gate))))
        ld_out[:, at[h]] = log_decay
        gf_out[:, at[h]] = speed * sigmoid(gate)
        both = lax.dot_general(
            tri, jnp.concatenate(split(log_decay), axis=1), NN, preferred_element_type=F32
        )
        cumul.append(both[:, :T] + both[:, T:])
        cum_out[:, at[h]] = cumul[h]
        betas.append(column(beta_all, base + h))
        acts = []
        for j, (raw, factor) in enumerate(((q_ref, fq_out), (k_ref, fk_out), (v_ref, fv_out))):
            ext[j, h, 0:8] = halo_ref[j, :, at[h]].astype(F32)
            ext[j, h, 8:136] = raw[:, at[h]].astype(F32)
            pre = conv_ref[j, 0:1, at[h]] * ext[j, h, 5 : 5 + T]
            for i in range(1, 4):
                pre = pre + conv_ref[j, i : i + 1, at[h]] * ext[j, h, 5 + i : 5 + i + T]
            s = sigmoid(pre)
            act = pre * s
            slope = s * (1.0 + pre * (1.0 - s))
            if j < 2:
                scale = lax.rsqrt(jnp.sum(act * act, axis=1, keepdims=True) + EPS)
                act = act * scale
                slope = slope * scale
            factor[:, at[h]] = slope
            acts.append(act)
        qs.append(acts[0])
        ks.append(acts[1])
        vs.append(acts[2])
        q_out[:, at[h]] = acts[0]
        k_out[:, at[h]] = acts[1]
    factors = [gate_factors(c) for c in cumul]
    couple, attend = [], []
    for h in each:
        up0, up1, down, full, end, last, late = factors[h]
        kd = ks[h] * down
        right = lanes(split(jnp.where(late, 0.0, kd)), split(jnp.where(late, kd, 0.0)))
        left = rows(
            lanes(split(ks[h] * up0), split(ks[h] * up1)), lanes(split(qs[h] * up0), split(qs[h] * up1))
        )
        both = dot(left, right, NT)
        couple.append(jnp.where(strict, both[:T], 0.0) * betas[h])
        attend.append(jnp.where(lower, both[T:], 0.0))
    inverse = unit_inverse(couple)
    for h in each:
        up0, up1, down, full, end, last, late = factors[h]
        inv_out[h] = inverse[h]
        both = dot(
            split(inverse[h]), lanes(split(betas[h] * ks[h] * full), split(betas[h] * vs[h])), NN
        )
        w, u = both[:, :T], both[:, T:]
        w_out[h] = w
        u_out[h] = u
        both = dot(split(ks[h] * end), split(both), TN)
        maps_ref[h, 0:T] = ident * last - both[:, :T]
        maps_ref[h, T : 2 * T] = both[:, T:]
        grad = (grad_ref[:, at[h]],)
        pg = dot(split(attend[h]), grad, TN)
        pg_out[h] = pg
        maps_ref[h, 2 * T : 3 * T] = dot(split(qs[h] * full), grad, TN) - dot(split(w), split(pg), TN)


def join(early, late):
    ea, eb, ed = early
    la, lb, ld = late
    sa = split(ea)
    both = dot(split(la), lanes(sa, split(eb)), NN)
    return (both[:, :T], both[:, T:] + lb, ed + dot(sa, split(ld), TN))


def tree(items):
    while len(items) > 1:
        items = [join(items[i], items[i + 1]) for i in range(0, len(items), 2)]
    return items[0]


def triple(ref, i):
    return tuple(ref[i, m * T : (m + 1) * T] for m in range(3))


def line_kernel(maps_ref, out_ref):
    total = tree([triple(maps_ref, i) for i in range(maps_ref.shape[0])])
    for m in range(3):
        out_ref[m * T : (m + 1) * T] = total[m]


def plane_kernel(where_ref, lines_ref, out_ref):
    count = lines_ref.shape[0]
    mine = where_ref[1]
    total = tree([triple(lines_ref, lax.rem(mine - i + count, count)) for i in range(count)])
    for m in range(3):
        out_ref[m * T : (m + 1) * T] = total[m]


def states_kernel(where_ref, maps_ref, lines_ref, planes_ref, out_ref):
    state = jnp.zeros((T, T), F32)
    grad = jnp.zeros((T, T), F32)
    for ref, mine in ((planes_ref, where_ref[0]), (lines_ref, where_ref[1])):
        count = ref.shape[0]
        for i in range(count - 1):
            slot = lax.rem(mine - i + count, count)
            a, b, d = triple(ref, slot)
            state = jnp.where(i < mine, dot(split(a), split(state), NN) + b, state)
            j = count - 1 - i
            slot = lax.rem(mine - j + count, count)
            a, b, d = triple(ref, slot)
            grad = jnp.where(j > mine, dot(split(a), split(grad), TN) + d, grad)
    count = maps_ref.shape[0]
    for i in range(count):
        j = count - 1 - i
        out_ref[i, 0:T] = state
        out_ref[j, T : 2 * T] = grad
        if i < count - 1:
            a, b, d = triple(maps_ref, i)
            state = dot(split(a), split(state), NN) + b
            a, b, d = triple(maps_ref, j)
            grad = dot(split(a), split(grad), TN) + d


def grads_kernel(
    heads,
    q_ref, k_ref, v_ref, halo_ref, beta_ref, conv_ref, grad_ref, states_ref,
    q_in, k_in, fq_in, fk_in, fv_in, cum_in, gf_in, ld_in, w_in, u_in, pg_in, inv_in,
    dq_out, dk_out, dv_out, edge_out, tail_out, dgate_out, dbeta_out, param_out,
    ext, back,
):
    row, col = iota((T, T), 0), iota((T, T), 1)
    strict = row > col
    lower = row >= col
    upper = jnp.where(row <= col, 1.0, 0.0).astype(BF16)
    ones = jnp.ones((8, T), BF16)
    beta_all = sigmoid(beta_ref[...])
    base = pl.program_id(0) * heads
    each = range(heads)
    at = [slice(h * T, (h + 1) * T) for h in each]
    deltas, dds, grads = [], [], []
    betas = [column(beta_all, base + h) for h in each]
    factors = [gate_factors(cum_in[:, at[h]]) for h in each]
    ms = [split(states_ref[h, 0:T]) for h in each]
    gs = [split(states_ref[h, T : 2 * T]) for h in each]
    qs = [q_in[:, at[h]] for h in each]
    ks = [k_in[:, at[h]] for h in each]
    dbeta = jnp.zeros(dbeta_out.shape, F32)
    for h in each:
        deltas.append(u_in[h] - dot(split(w_in[h]), ms[h], NN))
        dds.append(pg_in[h] + dot(split(ks[h] * factors[h][4]), gs[h], NN))
    des = [dot(split(inv_in[h]), split(dds[h]), TN) for h in each]
    dvs = [betas[h] * des[h] for h in each]
    dsp = [split(deltas[h]) for h in each]
    firsts = []
    for h in each:
        grad = grad_ref[:, at[h]]
        left = rows((grad, jnp.zeros_like(grad)), split(-dvs[h]))
        firsts.append(dot(left, rows(dsp[h], ms[h]), NT))
    ends = [dot(dsp[h], gs[h], NT) for h in each]
    for h in each:
        up0, up1, down, full, end, last, late = factors[h]
        q, k = qs[h], ks[h]
        first = firsts[h]
        sp = split(jnp.where(lower, first[:T, :T], 0.0))
        sl = split(jnp.where(strict, first[T:, :T], 0.0))
        kd = k * down
        right = lanes(split(jnp.where(late, 0.0, kd)), split(jnp.where(late, kd, 0.0)))
        by_row = dot(rows(sp, sl), right, NN)
        up = rows(lanes(split(k * up0), split(k * up1)), lanes(split(q * up0), split(q * up1)))
        by_col = dot(rows(sl, sp), up, TN)
        dq = full * first[:T, T:] + up0 * by_row[:T, :T] + up1 * by_row[:T, T:]
        dk_row = full * first[T:, T:] + up0 * by_row[T:, :T] + up1 * by_row[T:, T:]
        dk_end = end * ends[h]
        dk_col = down * jnp.where(late, by_col[:, T:], by_col[:, :T]) + dk_end
        dk = dk_row + dk_col
        dcum = q * dq + k * (dk_row - dk_col)
        held = states_ref[h, 0:T] * states_ref[h, T : 2 * T]
        dlast = jnp.sum(k * dk_end, axis=0, keepdims=True) + last * dot((ones,), split(held), NT)[0:1]
        both = lax.dot_general(
            upper, jnp.concatenate(split(dcum), axis=1), NN, preferred_element_type=F32
        )
        dlog = both[:, :T] + both[:, T:] + dlast
        dgate_out[:, at[h]] = dlog * gf_in[:, at[h]]
        param_out[12:13, at[h]] = jnp.sum(dlog * ld_in[:, at[h]], axis=0, keepdims=True)
        write = jnp.sum(des[h] * deltas[h], axis=1, keepdims=True) * (1.0 - betas[h])
        dbeta = jnp.where(iota(dbeta.shape, 1) == base + h, write, dbeta)
        pres = (
            fq_in[:, at[h]] * (dq - q * jnp.sum(q * dq, axis=1, keepdims=True)),
            fk_in[:, at[h]] * (dk - k * jnp.sum(k * dk, axis=1, keepdims=True)),
            fv_in[:, at[h]] * dvs[h],
        )
        for j, (raw, out) in enumerate(((q_ref, dq_out), (k_ref, dk_out), (v_ref, dv_out))):
            ext[j, h, 0:8] = halo_ref[j, :, at[h]].astype(F32)
            ext[j, h, 8:136] = raw[:, at[h]].astype(F32)
            back[j, h, 0:8] = jnp.zeros((8, T), F32)
            back[j, h, 8:136] = pres[j]
            back[j, h, 136:144] = jnp.zeros((8, T), F32)
            whole = None
            for i in range(4):
                part = conv_ref[j, i : i + 1, at[h]] * back[j, h, 3 - i : 3 - i + 136]
                whole = part if whole is None else whole + part
                param_out[4 * j + i : 4 * j + i + 1, at[h]] = jnp.sum(
                    pres[j] * ext[j, h, 5 + i : 5 + i + T], axis=0, keepdims=True
                )
            out[:, at[h]] = whole[8:136].astype(BF16)
            tail_out[j, :, at[h]] = whole[0:8]
            edge_out[j, :, at[h]] = whole[120:136]
    param_out[13:16] = jnp.zeros((3, heads * T), F32)

    @pl.when(pl.program_id(0) == 0)
    def _():
        dbeta_out[...] = dbeta

    @pl.when(pl.program_id(0) > 0)
    def _():
        dbeta_out[...] = dbeta_out[...] + dbeta


def per_device(query_raw, key_raw, value_raw, gate_raw, beta_raw, conv_weight, decay_log, grad_out):
    length, channels = gate_raw.shape
    count = beta_raw.shape[1]
    lines, planes = lax.axis_size("x"), lax.axis_size("y")
    depth = lax.axis_size("z")
    devices = lines * planes * depth
    heads = GROUP
    wide = heads * T
    wheres = jnp.stack([lax.axis_index("y"), lax.axis_index("x")]).astype(jnp.int32)
    ends = jnp.stack([query_raw[length - 8 :], key_raw[length - 8 :], value_raw[length - 8 :]])
    halo = lax.ppermute(ends, SEQ, [(i, i + 1) for i in range(devices - 1)])
    decay_row = decay_log.reshape(1, channels)

    tall = pl.BlockSpec((T, wide), lambda h: (0, h))
    edge = pl.BlockSpec((3, 8, wide), lambda h: (0, 0, h))
    taps = pl.BlockSpec((3, 4, wide), lambda h: (0, 0, h))
    beta_spec = pl.BlockSpec((T, count), lambda h: (0, 0))
    square = pl.BlockSpec((heads, T, T), lambda h: (h, 0, 0))

    def stack_spec(n):
        return pl.BlockSpec((heads, n * T, T), lambda h: (h, 0, 0))

    def like(*shape, dtype=F32):
        return jax.ShapeDtypeStruct(shape, dtype)

    params = pltpu.CompilerParams(
        dimension_semantics=("arbitrary",), vmem_limit_bytes=48 * MIB
    )
    saved_shapes = [like(length, channels)] * 8 + [like(count, T, T)] * 4
    saved_specs = [tall] * 8 + [square] * 4
    maps, *saved = pl.pallas_call(
        functools.partial(maps_kernel, heads),
        grid=(count // heads,),
        in_specs=[tall, tall, tall, edge, tall, beta_spec, taps, pl.BlockSpec((1, wide), lambda h: (0, h)), tall],
        out_specs=[stack_spec(3)] + saved_specs,
        out_shape=[like(count, 3 * T, T)] + saved_shapes,
        scratch_shapes=[pltpu.VMEM((3, heads, 136, T), F32)],
        compiler_params=params,
        name="block_maps",
    )(query_raw, key_raw, value_raw, halo, gate_raw, beta_raw, conv_weight, decay_row, grad_out)

    line_maps = lax.all_to_all(maps, "z", 0, 0, tiled=True)
    line_total = pl.pallas_call(
        line_kernel, out_shape=like(3 * T, T), name="line_total",
        compiler_params=pltpu.CompilerParams(vmem_limit_bytes=32 * MIB),
    )(line_maps)

    def around(block, axis):
        size = lax.axis_size(axis)
        moved = [
            lax.ppermute(block, axis, [(i, (i + d) % size) for i in range(size)])
            for d in range(1, size)
        ]
        return [block] + moved

    smem = pl.BlockSpec(memory_space=pltpu.SMEM)
    vmem = pl.BlockSpec(memory_space=pltpu.VMEM)
    line_totals = jnp.stack(around(line_total, "x"))
    plane_total = pl.pallas_call(
        plane_kernel, out_shape=like(3 * T, T), in_specs=[smem, vmem], name="plane_total",
        compiler_params=pltpu.CompilerParams(vmem_limit_bytes=32 * MIB),
    )(wheres, line_totals)
    plane_totals = jnp.stack(around(plane_total, "y"))
    line_states = pl.pallas_call(
        states_kernel, out_shape=like(depth, 2 * T, T), in_specs=[smem, vmem, vmem, vmem], name="line_states",
        compiler_params=pltpu.CompilerParams(vmem_limit_bytes=32 * MIB),
    )(wheres, line_maps, line_totals, plane_totals)
    states = lax.all_to_all(line_states, "z", 0, 0, tiled=True)

    dq, dk, dv, edges, tails, dgate, dbeta, partial = pl.pallas_call(
        functools.partial(grads_kernel, heads),
        grid=(count // heads,),
        in_specs=[tall, tall, tall, edge, beta_spec, taps, tall, stack_spec(2)] + saved_specs,
        out_specs=[
            tall, tall, tall,
            pl.BlockSpec((3, 16, wide), lambda h: (0, 0, h)), edge, tall, beta_spec,
            pl.BlockSpec((16, wide), lambda h: (0, h)),
        ],
        out_shape=[like(length, channels, dtype=BF16)] * 3
        + [like(3, 16, channels), like(3, 8, channels), like(length, channels), like(length, count), like(16, channels)],
        scratch_shapes=[pltpu.VMEM((3, heads, 136, T), F32), pltpu.VMEM((3, heads, 144, T), F32)],
        compiler_params=params,
        name="block_grads",
    )(query_raw, key_raw, value_raw, halo, beta_raw, conv_weight, grad_out, states, *saved)

    after = lax.ppermute(tails, SEQ, [(i + 1, i) for i in range(devices - 1)])
    fixed = edges + jnp.pad(after, ((0, 0), (8, 0), (0, 0)))

    def finish(full, extra):
        return lax.dynamic_update_slice(full, extra.astype(BF16), (length - 16, 0))

    total = partial
    for axis in ("x", "y"):
        own, one, two, three = around(total, axis)
        total = (own + two) + (one + three)
    for stride in (1, 2, 4):
        total = total + lax.ppermute(total, "z", [(i, i ^ stride) for i in range(depth)])
    return (
        finish(dq, fixed[0]),
        finish(dk, fixed[1]),
        finish(dv, fixed[2]),
        dgate,
        dbeta,
        total[:12].reshape(3, 4, channels),
        total[12],
    )


GROUP = 2


def solution(mesh):
    inner = Mesh(mesh.devices.reshape(4, 4, 8, 2), SEQ + ("head",))
    wide = P(SEQ, "head")
    in_specs = (wide, wide, wide, wide, wide, P(None, None, "head"), P("head"), wide)
    out_specs = (wide, wide, wide, wide, wide, P(None, None, "head"), P("head"))
    return jax.shard_map(
        per_device, mesh=inner, in_specs=in_specs, out_specs=out_specs, check_vma=False
    )
```

```python
import functools

import jax
import jax.numpy as jnp
from jax import lax
from jax.experimental import pallas as pl
from jax.experimental.pallas import tpu as pltpu
from jax.sharding import Mesh
from jax.sharding import PartitionSpec as P

F32 = jnp.float32
BF16 = jnp.bfloat16
EPS = 1e-06
T = 128
SEQ = ("y", "x", "z")
NN = (((1,), (0,)), ((), ()))
NT = (((1,), (1,)), ((), ()))
TN = (((0,), (0,)), ((), ()))
MIB = 1024 * 1024
AUX = 16
LINK = jnp.float16
TOP = 13.0
FLOOR = -200.0


def split(x):
    hi = x.astype(BF16)
    return (hi, (x - hi.astype(F32)).astype(BF16))


def dot(a, b, dims):
    total = None
    for i, left in enumerate(a):
        for j, right in enumerate(b):
            if i + j < 2:
                term = lax.dot_general(left, right, dims, preferred_element_type=F32)
                total = term if total is None else total + term
    return total


def lanes(*parts):
    return tuple(jnp.concatenate(terms, axis=1) for terms in zip(*parts))


def rows(*parts):
    return tuple(jnp.concatenate(terms, axis=0) for terms in zip(*parts))


def iota(shape, dim):
    return lax.broadcasted_iota(jnp.int32, shape, dim)


def sigmoid(x):
    return 1.0 / (1.0 + jnp.exp(-x))


def column(block, head):
    return jnp.sum(jnp.where(iota(block.shape, 1) == head, block, 0.0), axis=1, keepdims=True)


def gate_factors(cumul):
    row = iota((T, T), 0)
    late = row >= T // 2
    mid0 = cumul[T // 4 : T // 4 + 1]
    mid1 = cumul[3 * T // 4 : 3 * T // 4 + 1]
    last = cumul[T - 1 : T]
    up0 = jnp.exp(cumul - mid0)
    up1 = jnp.where(late, jnp.exp(jnp.where(late, cumul - mid1, 0.0)), 0.0)
    down = jnp.exp(jnp.where(late, mid1, mid0) - cumul)
    return up0, up1, down, jnp.exp(cumul), jnp.exp(last - cumul), jnp.exp(last), late


def unit_inverse(coupling):
    row, col = iota((T, T), 0), iota((T, T), 1)
    ident = jnp.where(row == col, 1.0, 0.0)

    def same(size):
        return (row // size) == (col // size)

    inner = [jnp.where(same(16), c, 0.0) for c in coupling]
    result = [ident - c for c in inner]
    power = []
    for c in inner:
        s = split(c)
        power.append(dot(s, s, NN))
    for level in range(2):
        out = []
        for p, r in zip(power, result):
            s = split(p)
            out.append(dot(rows(s, split(r)), s, NN))
        power = [o[:T] for o in out]
        result = [r + o[T:] for r, o in zip(result, out)]
    result = [r + dot(split(r), split(p), NN) for r, p in zip(result, power)]
    for size in (32, 64, 128):
        pick = same(size) & ~same(size // 2)
        parts = [split(r) for r in result]
        half = [dot(split(jnp.where(pick, c, 0.0)), s, NN) for c, s in zip(coupling, parts)]
        result = [r - dot(s, split(h), NN) for r, s, h in zip(result, parts, half)]
    return result


def maps_kernel(
    heads,
    q_ref, k_ref, v_ref, halo_ref, gate_ref, beta_ref, conv_ref, decay_ref, grad_ref,
    maps_ref, q_out, k_out, fq_out, fk_out, fv_out, cum_out, gf_out, ld_out, w_out, u_out, pg_out, inv_out,
    ext,
):
    row, col = iota((T, T), 0), iota((T, T), 1)
    strict = row > col
    lower = row >= col
    ident = jnp.where(row == col, 1.0, 0.0)
    tri = jnp.where(lower, 1.0, 0.0).astype(BF16)
    beta_all = sigmoid(beta_ref[...])
    base = pl.program_id(0) * heads
    each = range(heads)
    at = [slice(h * T, (h + 1) * T) for h in each]
    cumul, qs, ks, vs, betas = [], [], [], [], []
    for h in each:
        gate = gate_ref[:, at[h]]
        speed = -jnp.exp(decay_ref[:, at[h]])
        log_decay = speed * (jnp.maximum(gate, 0.0) + jnp.log1p(jnp.exp(-jnp.abs(gate))))
        ld_out[:, at[h]] = log_decay
        gf_out[:, at[h]] = speed * sigmoid(gate)
        both = lax.dot_general(
            tri, jnp.concatenate(split(log_decay), axis=1), NN, preferred_element_type=F32
        )
        cumul.append(both[:, :T] + both[:, T:])
        cum_out[:, at[h]] = cumul[h]
        betas.append(column(beta_all, base + h))
        acts = []
        for j, (raw, factor) in enumerate(((q_ref, fq_out), (k_ref, fk_out), (v_ref, fv_out))):
            ext[j, h, 0:8] = halo_ref[j, :, at[h]].astype(F32)
            ext[j, h, 8:136] = raw[:, at[h]].astype(F32)
            pre = conv_ref[j, 0:1, at[h]] * ext[j, h, 5 : 5 + T]
            for i in range(1, 4):
                pre = pre + conv_ref[j, i : i + 1, at[h]] * ext[j, h, 5 + i : 5 + i + T]
            s = sigmoid(pre)
            act = pre * s
            slope = s * (1.0 + pre * (1.0 - s))
            if j < 2:
                scale = lax.rsqrt(jnp.sum(act * act, axis=1, keepdims=True) + EPS)
                act = act * scale
                slope = slope * scale
            factor[:, at[h]] = slope
            acts.append(act)
        qs.append(acts[0])
        ks.append(acts[1])
        vs.append(acts[2])
        q_out[:, at[h]] = acts[0]
        k_out[:, at[h]] = acts[1]
    factors = [gate_factors(c) for c in cumul]
    couple, attend = [], []
    for h in each:
        up0, up1, down, full, end, last, late = factors[h]
        kd = ks[h] * down
        right = lanes(split(jnp.where(late, 0.0, kd)), split(jnp.where(late, kd, 0.0)))
        left = rows(
            lanes(split(ks[h] * up0), split(ks[h] * up1)), lanes(split(qs[h] * up0), split(qs[h] * up1))
        )
        both = dot(left, right, NT)
        couple.append(jnp.where(strict, both[:T], 0.0) * betas[h])
        attend.append(jnp.where(lower, both[T:], 0.0))
    inverse = unit_inverse(couple)
    for h in each:
        up0, up1, down, full, end, last, late = factors[h]
        inv_out[h] = inverse[h]
        both = dot(
            split(inverse[h]), lanes(split(betas[h] * ks[h] * full), split(betas[h] * vs[h])), NN
        )
        w, u = both[:, :T], both[:, T:]
        w_out[h] = w
        u_out[h] = u
        both = dot(split(ks[h] * end), split(both), TN)
        grad = (grad_ref[:, at[h]],)
        pg = dot(split(attend[h]), grad, TN)
        pg_out[h] = pg
        adjoint = dot(split(qs[h] * full), grad, TN) - dot(split(w), split(pg), TN)
        put(maps_ref.at[h], (-both[:, :T], both[:, T:], adjoint), cumul[h][T - 1 : T])


def put(ref, parts, log_decay):
    row = iota((AUX, T), 0)
    packed = jnp.zeros((AUX, T), F32)
    place = 0
    for i, square in enumerate(parts):
        largest = jnp.max(jnp.max(jnp.abs(square), axis=0, keepdims=True), axis=1, keepdims=True)
        power = jnp.floor(jnp.log2(jnp.maximum(largest, 1e-30)))
        ref[place : place + T] = square * jnp.exp2(TOP - power)
        packed = jnp.where(row == 3 + i, power, packed)
        place += T
    if log_decay is not None:
        rest = jnp.maximum(log_decay, FLOOR)
        for i in range(3):
            term = rest.astype(BF16).astype(F32)
            rest = rest - term
            packed = jnp.where(row == i, term, packed)
    ref[place : place + AUX] = packed


def get(ref):
    count = (ref.shape[0] - AUX) // T
    aux = ref[count * T : count * T + AUX]
    squares = [ref[m * T : (m + 1) * T] * jnp.exp2(aux[3 + m : 4 + m] - TOP) for m in range(count)]
    return (*squares, (aux[0:1] + aux[1:2]) + aux[2:3])


def whole_map(move, log_decay):
    row, col = iota((T, T), 0), iota((T, T), 1)
    return move + jnp.where(row == col, jnp.exp(log_decay), 0.0)


def join(early, late):
    ee, eb, ed, eg = early
    le, lb, ld, lg = late
    both = dot(split(whole_map(le, lg)), lanes(split(ee), split(eb)), NN)
    adjoint = ed + dot(split(whole_map(ee, eg)), split(ld), TN)
    return (both[:, :T] + le * jnp.exp(eg), both[:, T:] + lb, adjoint, eg + lg)


def tree(items):
    while len(items) > 1:
        items = [join(items[i], items[i + 1]) for i in range(0, len(items), 2)]
    return items[0]


def line_kernel(maps_ref, out_ref):
    *squares, log_decay = tree([get(maps_ref.at[i]) for i in range(maps_ref.shape[0])])
    put(out_ref, squares, log_decay)


def plane_kernel(where_ref, *refs):
    *lines, one, two, three, held = refs
    count = len(lines)
    mine, plane = where_ref[1], where_ref[0]
    for d, line in enumerate(lines):
        held[lax.rem(mine - d + count, count)] = line[...]
    move, offset, adjoint, log_decay = tree([get(held.at[i]) for i in range(count)])
    for d, out in enumerate((one, two, three)):
        put(out, (move, jnp.where(plane + d + 1 < count, offset, adjoint)), log_decay)


def advance(part, state, active):
    move, offset, log_decay = part
    new = dot(split(whole_map(move, log_decay)), split(state), NN) + offset
    return new if active is None else jnp.where(active, new, state)


def retreat(part, grad, active):
    move, adjoint, log_decay = part
    new = dot(split(whole_map(move, log_decay)), split(grad), TN) + adjoint
    return new if active is None else jnp.where(active, new, grad)


def states_kernel(where_ref, maps_ref, *refs):
    *moved, out_ref = refs
    lines, planes = moved[:3], moved[3:]
    state = jnp.zeros((T, T), F32)
    grad = jnp.zeros((T, T), F32)
    for refs, mine in ((planes, where_ref[0]), (lines, where_ref[1])):
        parts = [get(ref) for ref in refs]
        for i in range(3):
            part = parts[2 - i]
            state = advance((part[0], part[1], part[-1]), state, mine >= 3 - i)
            part = parts[i]
            grad = retreat((part[0], part[-2], part[-1]), grad, mine < i + 1)
    count = maps_ref.shape[0]
    states, grads = [state], [grad]
    for i in range(count - 1):
        move, offset, adjoint, log_decay = get(maps_ref.at[i])
        states.append(advance((move, offset, log_decay), states[-1], None))
        move, offset, adjoint, log_decay = get(maps_ref.at[count - 1 - i])
        grads.append(retreat((move, adjoint, log_decay), grads[-1], None))
    for i in range(count):
        put(out_ref.at[i], (states[i], grads[count - 1 - i]), None)


def grads_kernel(
    heads,
    q_ref, k_ref, v_ref, halo_ref, beta_ref, conv_ref, grad_ref, states_ref, where_ref,
    q_in, k_in, fq_in, fk_in, fv_in, cum_in, gf_in, ld_in, w_in, u_in, pg_in, inv_in,
    dq_out, dk_out, dv_out, edge_out, tail_out, dgate_out, dbeta_out, sum0_out, sum1_out, sum2_out, sum3_out,
    ext, back, params,
):
    row, col = iota((T, T), 0), iota((T, T), 1)
    strict = row > col
    lower = row >= col
    upper = jnp.where(row <= col, 1.0, 0.0).astype(BF16)
    ones = jnp.ones((8, T), BF16)
    beta_all = sigmoid(beta_ref[...])
    base = pl.program_id(0) * heads
    each = range(heads)
    at = [slice(h * T, (h + 1) * T) for h in each]
    deltas, dds, grads = [], [], []
    betas = [column(beta_all, base + h) for h in each]
    factors = [gate_factors(cum_in[:, at[h]]) for h in each]
    states = [get(states_ref.at[h]) for h in each]
    ms = [split(states[h][0]) for h in each]
    gs = [split(states[h][1]) for h in each]
    qs = [q_in[:, at[h]] for h in each]
    ks = [k_in[:, at[h]] for h in each]
    dbeta = jnp.zeros(dbeta_out.shape, F32)
    for h in each:
        deltas.append(u_in[h] - dot(split(w_in[h]), ms[h], NN))
        dds.append(pg_in[h] + dot(split(ks[h] * factors[h][4]), gs[h], NN))
    des = [dot(split(inv_in[h]), split(dds[h]), TN) for h in each]
    dvs = [betas[h] * des[h] for h in each]
    dsp = [split(deltas[h]) for h in each]
    firsts = []
    for h in each:
        grad = grad_ref[:, at[h]]
        left = rows((grad, jnp.zeros_like(grad)), split(-dvs[h]))
        both = [dot(left, dsp[h], NT), dot(left, ms[h], NT)]
        firsts.append(jnp.concatenate(both, axis=1))
    ends = [dot(dsp[h], gs[h], NT) for h in each]
    for h in each:
        up0, up1, down, full, end, last, late = factors[h]
        q, k = qs[h], ks[h]
        first = firsts[h]
        sp = split(jnp.where(lower, first[:T, :T], 0.0))
        sl = split(jnp.where(strict, first[T:, :T], 0.0))
        kd = k * down
        right = lanes(split(jnp.where(late, 0.0, kd)), split(jnp.where(late, kd, 0.0)))
        by_row = dot(rows(sp, sl), right, NN)
        up = rows(lanes(split(k * up0), split(k * up1)), lanes(split(q * up0), split(q * up1)))
        by_col = dot(rows(sl, sp), up, TN)
        dq = full * first[:T, T:] + up0 * by_row[:T, :T] + up1 * by_row[:T, T:]
        dk_row = full * first[T:, T:] + up0 * by_row[T:, :T] + up1 * by_row[T:, T:]
        dk_end = end * ends[h]
        dk_col = down * jnp.where(late, by_col[:, T:], by_col[:, :T]) + dk_end
        dk = dk_row + dk_col
        dcum = q * dq + k * (dk_row - dk_col)
        held = states[h][0] * states[h][1]
        dlast = jnp.sum(k * dk_end, axis=0, keepdims=True) + last * dot((ones,), split(held), NT)[0:1]
        both = lax.dot_general(
            upper, jnp.concatenate(split(dcum), axis=1), NN, preferred_element_type=F32
        )
        dlog = both[:, :T] + both[:, T:] + dlast
        dgate_out[:, at[h]] = dlog * gf_in[:, at[h]]
        params[base + h, 12:13] = jnp.sum(dlog * ld_in[:, at[h]], axis=0, keepdims=True)
        write = jnp.sum(des[h] * deltas[h], axis=1, keepdims=True) * (1.0 - betas[h])
        dbeta = jnp.where(iota(dbeta.shape, 1) == base + h, write, dbeta)
        pres = (
            fq_in[:, at[h]] * (dq - q * jnp.sum(q * dq, axis=1, keepdims=True)),
            fk_in[:, at[h]] * (dk - k * jnp.sum(k * dk, axis=1, keepdims=True)),
            fv_in[:, at[h]] * dvs[h],
        )
        for j, (raw, out) in enumerate(((q_ref, dq_out), (k_ref, dk_out), (v_ref, dv_out))):
            ext[j, h, 0:8] = halo_ref[j, :, at[h]].astype(F32)
            ext[j, h, 8:136] = raw[:, at[h]].astype(F32)
            back[j, h, 0:8] = jnp.zeros((8, T), F32)
            back[j, h, 8:136] = pres[j]
            back[j, h, 136:144] = jnp.zeros((8, T), F32)
            whole = None
            for i in range(4):
                part = conv_ref[j, i : i + 1, at[h]] * back[j, h, 3 - i : 3 - i + 136]
                whole = part if whole is None else whole + part
                params[base + h, 4 * j + i : 4 * j + i + 1] = jnp.sum(
                    pres[j] * ext[j, h, 5 + i : 5 + i + T], axis=0, keepdims=True
                )
            out[:, at[h]] = whole[8:136].astype(BF16)
            tail_out[j, :, at[h]] = whole[0:8]
            edge_out[j, :, at[h]] = whole[120:136]

    @pl.when(pl.program_id(0) == 0)
    def _():
        dbeta_out[...] = dbeta

    @pl.when(pl.program_id(0) > 0)
    def _():
        dbeta_out[...] = dbeta_out[...] + dbeta

    @pl.when(pl.program_id(0) == pl.num_programs(0) - 1)
    def _():
        for d, out in enumerate((sum0_out, sum1_out, sum2_out, sum3_out)):
            share = out.shape[0]
            out[:, 13:16] = jnp.zeros((share, 3, T), F32)
            for r in range(share):
                out[r, 0:13] = params[lax.rem(where_ref[1] + d, 4) * share + r, 0:13]


def gather_kernel(where_ref, *refs):
    *pieces, conv_out, decay_out, held = refs
    for d, piece in enumerate(pieces):
        held[lax.rem(where_ref[1] - d + 4, 4)] = piece[...]
    for p in range(4):
        for r in range(held.shape[1]):
            lane = (p * held.shape[1] + r) * T
            for j in range(3):
                conv_out[j, :, lane : lane + T] = held[p, r, 4 * j : 4 * j + 4]
            decay_out[:, lane : lane + T] = held[p, r, 12:13]


def widen(x):
    return x.astype(F32)


def per_device(query_raw, key_raw, value_raw, gate_raw, beta_raw, conv_weight, decay_log, grad_out):
    length, channels = gate_raw.shape
    count = beta_raw.shape[1]
    lines, planes = lax.axis_size("x"), lax.axis_size("y")
    depth = lax.axis_size("z")
    devices = lines * planes * depth
    heads = GROUP
    wide = heads * T
    wheres = jnp.stack([lax.axis_index("y"), lax.axis_index("x")]).astype(jnp.int32)
    ends = jnp.stack([query_raw[length - 8 :], key_raw[length - 8 :], value_raw[length - 8 :]])
    halo = lax.ppermute(ends, SEQ, [(i, i + 1) for i in range(devices - 1)])
    decay_row = decay_log.reshape(1, channels)

    tall = pl.BlockSpec((T, wide), lambda h: (0, h))
    edge = pl.BlockSpec((3, 8, wide), lambda h: (0, 0, h))
    taps = pl.BlockSpec((3, 4, wide), lambda h: (0, 0, h))
    beta_spec = pl.BlockSpec((T, count), lambda h: (0, 0))
    square = pl.BlockSpec((heads, T, T), lambda h: (h, 0, 0))

    def stack_spec(n):
        return pl.BlockSpec((heads, n * T, T), lambda h: (h, 0, 0))

    def like(*shape, dtype=F32):
        return jax.ShapeDtypeStruct(shape, dtype)

    params = pltpu.CompilerParams(
        dimension_semantics=("arbitrary",), vmem_limit_bytes=60 * MIB
    )
    saved_shapes = [like(length, channels)] * 8 + [like(count, T, T)] * 4
    saved_specs = [tall] * 8 + [square] * 4
    maps, *saved = pl.pallas_call(
        functools.partial(maps_kernel, heads),
        grid=(count // heads,),
        in_specs=[tall, tall, tall, edge, tall, beta_spec, taps, pl.BlockSpec((1, wide), lambda h: (0, h)), tall],
        out_specs=[pl.BlockSpec((heads, 3 * T + AUX, T), lambda h: (h, 0, 0))] + saved_specs,
        out_shape=[like(count, 3 * T + AUX, T)] + saved_shapes,
        scratch_shapes=[pltpu.VMEM((3, heads, 136, T), F32)],
        compiler_params=params,
        name="block_maps",
    )(query_raw, key_raw, value_raw, halo, gate_raw, beta_raw, conv_weight, decay_row, grad_out)

    line_maps = widen(lax.all_to_all(maps.astype(LINK), "z", 0, 0, tiled=True))
    small = pltpu.CompilerParams(vmem_limit_bytes=32 * MIB)
    line_total = pl.pallas_call(
        line_kernel, out_shape=like(3 * T + AUX, T), name="line_total", compiler_params=small
    )(line_maps)

    def around(blocks, axis):
        size = lax.axis_size(axis)
        return [
            lax.ppermute(block, axis, [(i, (i + d + 1) % size) for i in range(size)])
            for d, block in enumerate(blocks)
        ]

    smem = pl.BlockSpec(memory_space=pltpu.SMEM)
    vmem = pl.BlockSpec(memory_space=pltpu.VMEM)
    from_lines = [widen(x) for x in around([line_total.astype(LINK)] * 3, "x")]
    plane_totals = pl.pallas_call(
        plane_kernel, out_shape=[like(2 * T + AUX, T)] * 3, in_specs=[smem] + [vmem] * 4,
        scratch_shapes=[pltpu.VMEM((4, 3 * T + AUX, T), F32)], name="plane_total", compiler_params=small,
    )(wheres, line_total, *from_lines)
    from_planes = [widen(x) for x in around([x.astype(LINK) for x in plane_totals], "y")]
    line_states = pl.pallas_call(
        states_kernel, out_shape=like(depth, 2 * T + AUX, T), in_specs=[smem] + [vmem] * 7,
        name="line_states", compiler_params=small,
    )(wheres, line_maps, *from_lines, *from_planes)
    states = widen(lax.all_to_all(line_states.astype(LINK), "z", 0, 0, tiled=True))

    dq, dk, dv, edges, tails, dgate, dbeta, *sums = pl.pallas_call(
        functools.partial(grads_kernel, heads),
        grid=(count // heads,),
        in_specs=[
            tall, tall, tall, edge, beta_spec, taps, tall,
            pl.BlockSpec((heads, 2 * T + AUX, T), lambda h: (h, 0, 0)), smem,
        ] + saved_specs,
        out_specs=[
            tall, tall, tall,
            pl.BlockSpec((3, 16, wide), lambda h: (0, 0, h)), edge, tall, beta_spec,
        ] + [pl.BlockSpec((count // lines, 16, T), lambda h: (0, 0, 0))] * lines,
        out_shape=[like(length, channels, dtype=BF16)] * 3
        + [like(3, 16, channels), like(3, 8, channels), like(length, channels), like(length, count)] + [like(count // lines, 16, T)] * lines,
        scratch_shapes=[pltpu.VMEM((3, heads, 136, T), F32), pltpu.VMEM((3, heads, 144, T), F32), pltpu.VMEM((count, 16, T), F32)],
        compiler_params=params,
        name="block_grads",
    )(query_raw, key_raw, value_raw, halo, beta_raw, conv_weight, grad_out, states, wheres, *saved)

    after = lax.ppermute(tails.astype(BF16), SEQ, [(i + 1, i) for i in range(devices - 1)])
    fixed = edges + jnp.pad(after.astype(F32), ((0, 0), (8, 0), (0, 0)))

    def finish(full, extra):
        return lax.dynamic_update_slice(full, extra.astype(BF16), (length - 16, 0))

    one, two, three = around(sums[1:], "x")
    total = (sums[0] + one) + (two + three)
    one, two, three = around([total] * 3, "y")
    total = (total + two) + (one + three)
    two, four, six = [
        lax.ppermute(total, "z", [(i, (i + d) % depth) for i in range(depth)]) for d in (2, 4, 6)
    ]
    total = (total + four) + (two + six)
    total = total + lax.ppermute(total, "z", [(i, i ^ 1) for i in range(depth)])
    conv_sum, decay_sum = pl.pallas_call(
        gather_kernel, out_shape=[like(3, 4, channels), like(1, channels)], in_specs=[smem] + [vmem] * 4,
        scratch_shapes=[pltpu.VMEM((4, count // lines, 16, T), F32)], name="gather_sums", compiler_params=small,
    )(wheres, total, *around([total] * 3, "x"))
    return (
        finish(dq, fixed[0]),
        finish(dk, fixed[1]),
        finish(dv, fixed[2]),
        dgate,
        dbeta,
        conv_sum,
        decay_sum.reshape(channels),
    )


GROUP = 4


def solution(mesh):
    inner = Mesh(mesh.devices.reshape(4, 4, 8, 2), SEQ + ("head",))
    wide = P(SEQ, "head")
    in_specs = (wide, wide, wide, wide, wide, P(None, None, "head"), P("head"), wide)
    out_specs = (wide, wide, wide, wide, wide, P(None, None, "head"), P("head"))
    return jax.shard_map(
        per_device, mesh=inner, in_specs=in_specs, out_specs=out_specs, check_vma=False
    )
```

```python
import functools

import jax
import jax.numpy as jnp
from jax import lax
from jax.experimental import pallas as pl
from jax.experimental.pallas import tpu as pltpu
from jax.sharding import Mesh
from jax.sharding import PartitionSpec as P

F32 = jnp.float32
BF16 = jnp.bfloat16
EPS = 1e-06
T = 128
SEQ = ("y", "x", "z")
NN = (((1,), (0,)), ((), ()))
NT = (((1,), (1,)), ((), ()))
TN = (((0,), (0,)), ((), ()))
MIB = 1024 * 1024
AUX = 16
WIDEST = 128
LINK = jnp.float16
TOP = 13.0
FLOOR = -200.0


def split(x):
    hi = x.astype(BF16)
    return (hi, (x - hi.astype(F32)).astype(BF16))


def dot(a, b, dims):
    (left_dim,), (right_dim,) = dims[0]
    width = b[0].shape[1 - right_dim]

    def run(left, right):
        return lax.dot_general(left, right, dims, preferred_element_type=F32)

    if len(a) == 1 and len(b) == 1:
        return run(a[0], b[0])
    if len(b) == 1:
        return run(jnp.concatenate(a, axis=left_dim), jnp.concatenate([b[0]] * 2, axis=right_dim))
    if len(a) == 1:
        both = run(a[0], jnp.concatenate(b, axis=1 - right_dim))
        return both[:, :width] + both[:, width:]
    left = jnp.concatenate(a, axis=left_dim)
    right = jnp.concatenate([b[0]] * 2, axis=right_dim)
    if width > WIDEST:
        return run(left, right) + run(a[0], b[1])
    low = jnp.concatenate([b[1]] * 2, axis=right_dim)
    both = run(left, jnp.concatenate([right, low], axis=1 - right_dim))
    return both[:, :width] + both[:, width:]


def lanes(*parts):
    return tuple(jnp.concatenate(terms, axis=1) for terms in zip(*parts))


def rows(*parts):
    return tuple(jnp.concatenate(terms, axis=0) for terms in zip(*parts))


def iota(shape, dim):
    return lax.broadcasted_iota(jnp.int32, shape, dim)


def sigmoid(x):
    return 1.0 / (1.0 + jnp.exp(-x))


def column(ref, head):
    square = iota((T, T), 0) == iota((T, T), 1)
    return jnp.sum(jnp.where(square, sigmoid(ref[pl.ds(head, 1)]), 0.0), axis=1, keepdims=True)


def gate_factors(cumul):
    row = iota((T, T), 0)
    late = row >= T // 2
    mid0 = cumul[T // 4 : T // 4 + 1]
    mid1 = cumul[3 * T // 4 : 3 * T // 4 + 1]
    last = cumul[T - 1 : T]
    up0 = jnp.exp(cumul - mid0)
    up1 = jnp.where(late, jnp.exp(jnp.where(late, cumul - mid1, 0.0)), 0.0)
    down = jnp.exp(jnp.where(late, mid1, mid0) - cumul)
    return up0, up1, down, jnp.exp(cumul), jnp.exp(last - cumul), jnp.exp(last), late


def unit_inverse(coupling):
    row, col = iota((T, T), 0), iota((T, T), 1)
    ident = jnp.where(row == col, 1.0, 0.0)

    def same(size):
        return (row // size) == (col // size)

    inner = [jnp.where(same(16), c, 0.0) for c in coupling]
    result = [ident - c for c in inner]
    power = []
    for c in inner:
        s = split(c)
        power.append(dot(s, s, NN))
    for level in range(2):
        out = []
        for p, r in zip(power, result):
            s = split(p)
            out.append(dot(rows(s, split(r)), s, NN))
        power = [o[:T] for o in out]
        result = [r + o[T:] for r, o in zip(result, out)]
    result = [r + dot(split(r), split(p), NN) for r, p in zip(result, power)]
    for size in (32, 64, 128):
        pick = same(size) & ~same(size // 2)
        parts = [split(r) for r in result]
        half = [dot(split(jnp.where(pick, c, 0.0)), s, NN) for c, s in zip(coupling, parts)]
        result = [r - dot(s, split(h), NN) for r, s, h in zip(result, parts, half)]
    return result


def maps_kernel(
    heads,
    q_ref, k_ref, v_ref, halo_ref, gate_ref, beta_ref, conv_ref, decay_ref, grad_ref,
    maps_ref, q_out, k_out, fq_out, fk_out, fv_out, cum_out, gf_out, ld_out, w_out, u_out, pg_out, inv_out,
    ext,
):
    row, col = iota((T, T), 0), iota((T, T), 1)
    strict = row > col
    lower = row >= col
    ident = jnp.where(row == col, 1.0, 0.0)
    tri = jnp.where(lower, 1.0, 0.0).astype(BF16)
    base = pl.program_id(0) * heads
    each = range(heads)
    at = [slice(h * T, (h + 1) * T) for h in each]
    cumul, qs, ks, vs, betas = [], [], [], [], []
    for h in each:
        gate = gate_ref[:, at[h]]
        speed = -jnp.exp(decay_ref[:, at[h]])
        log_decay = speed * (jnp.maximum(gate, 0.0) + jnp.log1p(jnp.exp(-jnp.abs(gate))))
        ld_out[:, at[h]] = log_decay
        gf_out[:, at[h]] = speed * sigmoid(gate)
        both = lax.dot_general(
            tri, jnp.concatenate(split(log_decay), axis=1), NN, preferred_element_type=F32
        )
        cumul.append(both[:, :T] + both[:, T:])
        cum_out[:, at[h]] = cumul[h]
        betas.append(column(beta_ref, base + h))
        acts = []
        for j, (raw, factor) in enumerate(((q_ref, fq_out), (k_ref, fk_out), (v_ref, fv_out))):
            ext[j, h, 5:8] = halo_ref[:, at[h]].astype(F32)[3 * j : 3 * j + 3]
            ext[j, h, 8:136] = raw[:, at[h]].astype(F32)
            pre = conv_ref[j, 0:1, at[h]] * ext[j, h, 5 : 5 + T]
            for i in range(1, 4):
                pre = pre + conv_ref[j, i : i + 1, at[h]] * ext[j, h, 5 + i : 5 + i + T]
            s = sigmoid(pre)
            act = pre * s
            slope = s * (1.0 + pre * (1.0 - s))
            if j < 2:
                scale = lax.rsqrt(jnp.sum(act * act, axis=1, keepdims=True) + EPS)
                act = act * scale
                slope = slope * scale
            factor[:, at[h]] = slope
            acts.append(act)
        qs.append(acts[0])
        ks.append(acts[1])
        vs.append(acts[2])
        q_out[:, at[h]] = acts[0]
        k_out[:, at[h]] = acts[1]
    factors = [gate_factors(c) for c in cumul]
    couple, attend = [], []
    for h in each:
        up0, up1, down, full, end, last, late = factors[h]
        kd = ks[h] * down
        right = lanes(split(jnp.where(late, 0.0, kd)), split(jnp.where(late, kd, 0.0)))
        left = rows(
            lanes(split(ks[h] * up0), split(ks[h] * up1)), lanes(split(qs[h] * up0), split(qs[h] * up1))
        )
        both = dot(left, right, NT)
        couple.append(jnp.where(strict, both[:T], 0.0) * betas[h])
        attend.append(jnp.where(lower, both[T:], 0.0))
    inverse = unit_inverse(couple)
    for h in each:
        up0, up1, down, full, end, last, late = factors[h]
        inv_out[h] = inverse[h]
        both = dot(
            split(inverse[h]), lanes(split(betas[h] * ks[h] * full), split(betas[h] * vs[h])), NN
        )
        w, u = both[:, :T], both[:, T:]
        w_out[h] = w
        u_out[h] = u
        both = dot(split(ks[h] * end), split(both), TN)
        grad = (grad_ref[:, at[h]],)
        pg = dot(split(attend[h]), grad, TN)
        pg_out[h] = pg
        adjoint = dot(split(qs[h] * full), grad, TN) - dot(split(w), split(pg), TN)
        put(maps_ref.at[h], (-both[:, :T], both[:, T:], adjoint), cumul[h][T - 1 : T])


def put(ref, parts, log_decay):
    row = iota((AUX, T), 0)
    packed = jnp.zeros((AUX, T), F32)
    place = 0
    for i, square in enumerate(parts):
        largest = jnp.max(jnp.max(jnp.abs(square), axis=0, keepdims=True), axis=1, keepdims=True)
        power = jnp.floor(jnp.log2(jnp.maximum(largest, 1e-30)))
        ref[place : place + T] = square * jnp.exp2(TOP - power)
        packed = jnp.where(row == 3 + i, power, packed)
        place += T
    if log_decay is not None:
        rest = jnp.maximum(log_decay, FLOOR)
        for i in range(3):
            term = rest.astype(BF16).astype(F32)
            rest = rest - term
            packed = jnp.where(row == i, term, packed)
    ref[place : place + AUX] = packed


def get(ref):
    count = (ref.shape[0] - AUX) // T
    aux = ref[count * T : count * T + AUX]
    squares = [ref[m * T : (m + 1) * T] * jnp.exp2(aux[3 + m : 4 + m] - TOP) for m in range(count)]
    return (*squares, (aux[0:1] + aux[1:2]) + aux[2:3])


def whole_map(move, log_decay):
    row, col = iota((T, T), 0), iota((T, T), 1)
    return move + jnp.where(row == col, jnp.exp(log_decay), 0.0)


def join(early, late):
    ee, eb, ed, eg = early
    le, lb, ld, lg = late
    both = dot(split(whole_map(le, lg)), lanes(split(ee), split(eb)), NN)
    adjoint = ed + dot(split(whole_map(ee, eg)), split(ld), TN)
    return (both[:, :T] + le * jnp.exp(eg), both[:, T:] + lb, adjoint, eg + lg)


def tree(items):
    while len(items) > 1:
        items = [join(items[i], items[i + 1]) for i in range(0, len(items), 2)]
    return items[0]


def line_kernel(maps_ref, out_ref):
    *squares, log_decay = tree([get(maps_ref.at[i]) for i in range(maps_ref.shape[0])])
    put(out_ref, squares, log_decay)


def plane_kernel(where_ref, *refs):
    *lines, one, two, three, held = refs
    count = len(lines)
    mine, plane = where_ref[1], where_ref[0]
    for d, line in enumerate(lines):
        held[lax.rem(mine - d + count, count)] = line[...]
    move, offset, adjoint, log_decay = tree([get(held.at[i]) for i in range(count)])
    for d, out in enumerate((one, two, three)):
        put(out, (move, jnp.where(plane + d + 1 < count, offset, adjoint)), log_decay)


def advance(part, state, active):
    move, offset, log_decay = part
    new = dot(split(whole_map(move, log_decay)), split(state), NN) + offset
    return new if active is None else jnp.where(active, new, state)


def retreat(part, grad, active):
    move, adjoint, log_decay = part
    new = dot(split(whole_map(move, log_decay)), split(grad), TN) + adjoint
    return new if active is None else jnp.where(active, new, grad)


def states_kernel(where_ref, maps_ref, *refs):
    *moved, out_ref = refs
    lines, planes = moved[:3], moved[3:]
    state = jnp.zeros((T, T), F32)
    grad = jnp.zeros((T, T), F32)
    for refs, mine in ((planes, where_ref[0]), (lines, where_ref[1])):
        parts = [get(ref) for ref in refs]
        for i in range(3):
            part = parts[2 - i]
            state = advance((part[0], part[1], part[-1]), state, mine >= 3 - i)
            part = parts[i]
            grad = retreat((part[0], part[-2], part[-1]), grad, mine < i + 1)
    count = maps_ref.shape[0]
    states, grads = [state], [grad]
    for i in range(count - 1):
        move, offset, adjoint, log_decay = get(maps_ref.at[i])
        states.append(advance((move, offset, log_decay), states[-1], None))
        move, offset, adjoint, log_decay = get(maps_ref.at[count - 1 - i])
        grads.append(retreat((move, adjoint, log_decay), grads[-1], None))
    for i in range(count):
        put(out_ref.at[i], (states[i], grads[count - 1 - i]), None)


def grads_kernel(
    heads,
    q_ref, k_ref, v_ref, halo_ref, beta_ref, conv_ref, grad_ref, states_ref,
    q_in, k_in, fq_in, fk_in, fv_in, cum_in, gf_in, ld_in, w_in, u_in, pg_in, inv_in,
    dq_out, dk_out, dv_out, edge_out, tail_out, dgate_out, dbeta_out, params,
    ext, back, tail,
):
    row, col = iota((T, T), 0), iota((T, T), 1)
    strict = row > col
    lower = row >= col
    upper = jnp.where(row <= col, 1.0, 0.0).astype(BF16)
    ones = jnp.ones((8, T), BF16)
    tail[9:16] = jnp.zeros((7, T), F32)
    base = pl.program_id(0) * heads
    each = range(heads)
    at = [slice(h * T, (h + 1) * T) for h in each]
    deltas, dds, grads = [], [], []
    betas = [column(beta_ref, base + h) for h in each]
    factors = [gate_factors(cum_in[:, at[h]]) for h in each]
    states = [get(states_ref.at[h]) for h in each]
    ms = [split(states[h][0]) for h in each]
    gs = [split(states[h][1]) for h in each]
    qs = [q_in[:, at[h]] for h in each]
    ks = [k_in[:, at[h]] for h in each]
    for h in each:
        params[h, 13:16] = jnp.zeros((3, T), F32)
    for h in each:
        deltas.append(u_in[h] - dot(split(w_in[h]), ms[h], NN))
        dds.append(pg_in[h] + dot(split(ks[h] * factors[h][4]), gs[h], NN))
    des = [dot(split(inv_in[h]), split(dds[h]), TN) for h in each]
    dvs = [betas[h] * des[h] for h in each]
    dsp = [split(deltas[h]) for h in each]
    firsts = []
    for h in each:
        grad = grad_ref[:, at[h]]
        left = rows((grad, jnp.zeros_like(grad)), split(-dvs[h]))
        both = [dot(left, dsp[h], NT), dot(left, ms[h], NT)]
        firsts.append(jnp.concatenate(both, axis=1))
    ends = [dot(dsp[h], gs[h], NT) for h in each]
    for h in each:
        up0, up1, down, full, end, last, late = factors[h]
        q, k = qs[h], ks[h]
        first = firsts[h]
        sp = split(jnp.where(lower, first[:T, :T], 0.0))
        sl = split(jnp.where(strict, first[T:, :T], 0.0))
        kd = k * down
        right = lanes(split(jnp.where(late, 0.0, kd)), split(jnp.where(late, kd, 0.0)))
        by_row = dot(rows(sp, sl), right, NN)
        up = rows(lanes(split(k * up0), split(k * up1)), lanes(split(q * up0), split(q * up1)))
        by_col = dot(rows(sl, sp), up, TN)
        dq = full * first[:T, T:] + up0 * by_row[:T, :T] + up1 * by_row[:T, T:]
        dk_row = full * first[T:, T:] + up0 * by_row[T:, :T] + up1 * by_row[T:, T:]
        dk_end = end * ends[h]
        dk_col = down * jnp.where(late, by_col[:, T:], by_col[:, :T]) + dk_end
        dk = dk_row + dk_col
        dcum = q * dq + k * (dk_row - dk_col)
        held = states[h][0] * states[h][1]
        dlast = jnp.sum(k * dk_end, axis=0, keepdims=True) + last * dot((ones,), split(held), NT)[0:1]
        both = lax.dot_general(
            upper, jnp.concatenate(split(dcum), axis=1), NN, preferred_element_type=F32
        )
        dlog = both[:, :T] + both[:, T:] + dlast
        dgate_out[:, at[h]] = dlog * gf_in[:, at[h]]
        params[h, 12:13] = jnp.sum(dlog * ld_in[:, at[h]], axis=0, keepdims=True)
        write = jnp.sum(des[h] * deltas[h], axis=1, keepdims=True) * (1.0 - betas[h])
        dbeta_out[pl.ds(base + h, 1)] = jnp.sum(jnp.where(row == col, write, 0.0), axis=0, keepdims=True)
        pres = (
            fq_in[:, at[h]] * (dq - q * jnp.sum(q * dq, axis=1, keepdims=True)),
            fk_in[:, at[h]] * (dk - k * jnp.sum(k * dk, axis=1, keepdims=True)),
            fv_in[:, at[h]] * dvs[h],
        )
        for j, (raw, out) in enumerate(((q_ref, dq_out), (k_ref, dk_out), (v_ref, dv_out))):
            ext[j, h, 5:8] = halo_ref[:, at[h]].astype(F32)[3 * j : 3 * j + 3]
            ext[j, h, 8:136] = raw[:, at[h]].astype(F32)
            back[j, h, 0:8] = jnp.zeros((8, T), F32)
            back[j, h, 8:136] = pres[j]
            back[j, h, 136:144] = jnp.zeros((8, T), F32)
            whole = None
            for i in range(4):
                part = conv_ref[j, i : i + 1, at[h]] * back[j, h, 3 - i : 3 - i + 136]
                whole = part if whole is None else whole + part
                params[h, 4 * j + i : 4 * j + i + 1] = jnp.sum(
                    pres[j] * ext[j, h, 5 + i : 5 + i + T], axis=0, keepdims=True
                )
            out[:, at[h]] = whole[8:136].astype(BF16)
            tail[3 * j : 3 * j + 3] = whole[5:8]
            edge_out[j, :, at[h]] = whole[120:136]
        tail_out[:, at[h]] = tail[...].astype(BF16)


def ends_kernel(q_ref, k_ref, v_ref, out_ref):
    row = iota(out_ref.shape, 0)
    packed = jnp.zeros(out_ref.shape, F32)
    for j, ref in enumerate((q_ref, k_ref, v_ref)):
        turned = pltpu.roll(ref[...].astype(F32), 3 * j + 3, axis=0)
        packed = jnp.where((row >= 3 * j) & (row < 3 * j + 3), turned, packed)
    out_ref[...] = packed.astype(BF16)


def share_kernel(parts_ref, out_ref):
    total = parts_ref[0]
    for i in range(1, parts_ref.shape[0]):
        total = total + parts_ref[i]
    for i in range(out_ref.shape[0]):
        out_ref[i] = total


def gather_kernel(parts_ref, conv_out, decay_out):
    for h in range(parts_ref.shape[0]):
        lane = slice(h * T, (h + 1) * T)
        for j in range(3):
            conv_out[j, :, lane] = parts_ref[h, 4 * j : 4 * j + 4]
        decay_out[:, lane] = parts_ref[h, 12:13]


def widen(x):
    return x.astype(F32)


def per_device(query_raw, key_raw, value_raw, gate_raw, beta_raw, conv_weight, decay_log, grad_out):
    length, channels = gate_raw.shape
    count = beta_raw.shape[1]
    lines, planes = lax.axis_size("x"), lax.axis_size("y")
    depth = lax.axis_size("z")
    devices = lines * planes * depth
    wheres = jnp.stack([lax.axis_index("y"), lax.axis_index("x")]).astype(jnp.int32)
    ends = pl.pallas_call(
        ends_kernel, grid=(1,), out_shape=jax.ShapeDtypeStruct((16, channels), BF16),
        in_specs=[pl.BlockSpec((16, channels), lambda i: (length // 16 - 1, 0))] * 3,
        out_specs=pl.BlockSpec((16, channels), lambda i: (0, 0)), name="last_rows",
        compiler_params=pltpu.CompilerParams(vmem_limit_bytes=60 * MIB),
    )(query_raw, key_raw, value_raw)
    halo = lax.ppermute(ends, SEQ, [(i, i + 1) for i in range(devices - 1)])
    decay_row = decay_log.reshape(1, channels)

    def specs(heads):
        wide = heads * T
        return (
            pl.BlockSpec((T, wide), lambda h: (0, h)),
            pl.BlockSpec((16, wide), lambda h: (0, h)),
            pl.BlockSpec((3, 4, wide), lambda h: (0, 0, h)),
            pl.BlockSpec((count, T), lambda h: (0, 0)),
            pl.BlockSpec((heads, T, T), lambda h: (h, 0, 0)),
        )

    def like(*shape, dtype=F32):
        return jax.ShapeDtypeStruct(shape, dtype)

    params = pltpu.CompilerParams(
        dimension_semantics=("arbitrary",), vmem_limit_bytes=60 * MIB
    )
    saved_shapes = [like(length, channels)] * 8 + [like(count, T, T)] * 4
    heads = MAPS_GROUP
    wide = heads * T
    tall, edge, taps, beta_spec, square = specs(heads)
    saved_specs = [tall] * 8 + [square] * 4
    maps, *saved = pl.pallas_call(
        functools.partial(maps_kernel, heads),
        grid=(count // heads,),
        in_specs=[tall, tall, tall, edge, tall, beta_spec, taps, pl.BlockSpec((1, wide), lambda h: (0, h)), tall],
        out_specs=[pl.BlockSpec((heads, 3 * T + AUX, T), lambda h: (h, 0, 0))] + saved_specs,
        out_shape=[like(count, 3 * T + AUX, T)] + saved_shapes,
        scratch_shapes=[pltpu.VMEM((3, heads, 136, T), F32)],
        compiler_params=params,
        name="block_maps",
    )(query_raw, key_raw, value_raw, halo, gate_raw, beta_raw.T, conv_weight, decay_row, grad_out)

    line_maps = widen(lax.all_to_all(maps.astype(LINK), "z", 0, 0, tiled=True))
    small = pltpu.CompilerParams(vmem_limit_bytes=32 * MIB)
    line_total = pl.pallas_call(
        line_kernel, out_shape=like(3 * T + AUX, T), name="line_total", compiler_params=small
    )(line_maps)

    def around(blocks, axis):
        size = lax.axis_size(axis)
        return [
            lax.ppermute(block, axis, [(i, (i + d + 1) % size) for i in range(size)])
            for d, block in enumerate(blocks)
        ]

    smem = pl.BlockSpec(memory_space=pltpu.SMEM)
    vmem = pl.BlockSpec(memory_space=pltpu.VMEM)
    from_lines = [widen(x) for x in around([line_total.astype(LINK)] * 3, "x")]
    plane_totals = pl.pallas_call(
        plane_kernel, out_shape=[like(2 * T + AUX, T)] * 3, in_specs=[smem] + [vmem] * 4,
        scratch_shapes=[pltpu.VMEM((4, 3 * T + AUX, T), F32)], name="plane_total", compiler_params=small,
    )(wheres, line_total, *from_lines)
    from_planes = [widen(x) for x in around([x.astype(LINK) for x in plane_totals], "y")]
    line_states = pl.pallas_call(
        states_kernel, out_shape=like(depth, 2 * T + AUX, T), in_specs=[smem] + [vmem] * 7,
        name="line_states", compiler_params=small,
    )(wheres, line_maps, *from_lines, *from_planes)
    states = widen(lax.all_to_all(line_states.astype(LINK), "z", 0, 0, tiled=True))

    heads = GRADS_GROUP
    wide = heads * T
    tall, edge, taps, beta_spec, square = specs(heads)
    saved_specs = [tall] * 8 + [square] * 4
    dq, dk, dv, edges, tails, dgate, dbeta, sums = pl.pallas_call(
        functools.partial(grads_kernel, heads),
        grid=(count // heads,),
        in_specs=[
            tall, tall, tall, edge, beta_spec, taps, tall,
            pl.BlockSpec((heads, 2 * T + AUX, T), lambda h: (h, 0, 0)),
        ] + saved_specs,
        out_specs=[
            tall, tall, tall,
            pl.BlockSpec((3, 16, wide), lambda h: (0, 0, h)), edge, tall, beta_spec,
            pl.BlockSpec((heads, 16, T), lambda h: (h, 0, 0)),
        ],
        out_shape=[like(length, channels, dtype=BF16)] * 3
        + [like(3, 16, channels), like(16, channels, dtype=BF16), like(length, channels), like(count, length), like(count, 16, T)],
        scratch_shapes=[pltpu.VMEM((3, heads, 136, T), F32), pltpu.VMEM((3, heads, 144, T), F32), pltpu.VMEM((16, T), F32)],
        compiler_params=params,
        name="block_grads",
    )(query_raw, key_raw, value_raw, halo, beta_raw.T, conv_weight, grad_out, states, *saved)

    after = lax.ppermute(tails, SEQ, [(i + 1, i) for i in range(devices - 1)])
    def finish(full, extra):
        return lax.dynamic_update_slice(full, extra.astype(BF16), (length - 16, 0))


    def share(parts, copies):
        return pl.pallas_call(
            share_kernel, out_shape=like(copies, 16, T), name="share_sums", compiler_params=small
        )(parts)

    across = ("y", "x")
    sums = share(lax.all_to_all(sums, "z", 0, 0, tiled=True), lines * planes)
    sums = share(lax.all_to_all(sums, across, 0, 0, tiled=True), depth)
    sums, after = lax.optimization_barrier((sums, after))
    fixed = edges + jnp.pad(after[:9].astype(F32).reshape(3, 3, channels), ((0, 0), (13, 0), (0, 0)))

    conv_sum, decay_sum = pl.pallas_call(
        gather_kernel, out_shape=[like(3, 4, channels), like(1, channels)],
        name="gather_sums", compiler_params=small,
    )(lax.all_to_all(sums, "z", 0, 0, tiled=True))
    return (
        finish(dq, fixed[0]),
        finish(dk, fixed[1]),
        finish(dv, fixed[2]),
        dgate,
        dbeta.T,
        conv_sum,
        decay_sum.reshape(channels),
    )


MAPS_GROUP = 8
GRADS_GROUP = 4


def solution(mesh):
    inner = Mesh(mesh.devices.reshape(4, 4, 8, 2), SEQ + ("head",))
    wide = P(SEQ, "head")
    in_specs = (wide, wide, wide, wide, wide, P(None, None, "head"), P("head"), wide)
    out_specs = (wide, wide, wide, wide, wide, P(None, None, "head"), P("head"))
    return jax.shard_map(
        per_device, mesh=inner, in_specs=in_specs, out_specs=out_specs, check_vma=False
    )
```

```python
import functools

import jax
import jax.numpy as jnp
from jax import lax
from jax.experimental import pallas as pl
from jax.experimental.pallas import tpu as pltpu
from jax.sharding import Mesh
from jax.sharding import PartitionSpec as P

F32 = jnp.float32
BF16 = jnp.bfloat16
EPS = 1e-06
T = 128
SEQ = ("y", "x", "z")
NN = (((1,), (0,)), ((), ()))
NT = (((1,), (1,)), ((), ()))
TN = (((0,), (0,)), ((), ()))
MIB = 1024 * 1024
AUX = 16
WIDEST = 128
LINK = jnp.float16
TOP = 13.0
FLOOR = -200.0


def split(x):
    hi = x.astype(BF16)
    return (hi, (x - hi.astype(F32)).astype(BF16))


def dot(a, b, dims):
    (left_dim,), (right_dim,) = dims[0]
    width = b[0].shape[1 - right_dim]

    def run(left, right):
        return lax.dot_general(left, right, dims, preferred_element_type=F32)

    if len(a) == 1 and len(b) == 1:
        return run(a[0], b[0])
    if len(b) == 1:
        return run(jnp.concatenate(a, axis=left_dim), jnp.concatenate([b[0]] * 2, axis=right_dim))
    if len(a) == 1:
        both = run(a[0], jnp.concatenate(b, axis=1 - right_dim))
        return both[:, :width] + both[:, width:]
    left = jnp.concatenate(a, axis=left_dim)
    right = jnp.concatenate([b[0]] * 2, axis=right_dim)
    if width > WIDEST:
        return run(left, right) + run(a[0], b[1])
    low = jnp.concatenate([b[1]] * 2, axis=right_dim)
    both = run(left, jnp.concatenate([right, low], axis=1 - right_dim))
    return both[:, :width] + both[:, width:]


def lanes(*parts):
    return tuple(jnp.concatenate(terms, axis=1) for terms in zip(*parts))


def rows(*parts):
    return tuple(jnp.concatenate(terms, axis=0) for terms in zip(*parts))


def iota(shape, dim):
    return lax.broadcasted_iota(jnp.int32, shape, dim)


def sigmoid(x):
    return 1.0 / (1.0 + jnp.exp(-x))


def column(ref, head):
    square = iota((T, T), 0) == iota((T, T), 1)
    return jnp.sum(jnp.where(square, sigmoid(ref[pl.ds(head, 1)]), 0.0), axis=1, keepdims=True)


def gate_factors(cumul):
    row = iota((T, T), 0)
    late = row >= T // 2
    mid0 = cumul[T // 4 : T // 4 + 1]
    mid1 = cumul[3 * T // 4 : 3 * T // 4 + 1]
    last = cumul[T - 1 : T]
    up0 = jnp.exp(cumul - mid0)
    up1 = jnp.where(late, jnp.exp(jnp.where(late, cumul - mid1, 0.0)), 0.0)
    down = jnp.exp(jnp.where(late, mid1, mid0) - cumul)
    return up0, up1, down, jnp.exp(cumul), jnp.exp(last - cumul), jnp.exp(last), late


def unit_inverse(coupling):
    row, col = iota((T, T), 0), iota((T, T), 1)
    ident = jnp.where(row == col, 1.0, 0.0)

    def same(size):
        return (row // size) == (col // size)

    inner = [jnp.where(same(16), c, 0.0) for c in coupling]
    result = [ident - c for c in inner]
    power = []
    for c in inner:
        s = split(c)
        power.append(dot(s, s, NN))
    for level in range(2):
        out = []
        for p, r in zip(power, result):
            s = split(p)
            out.append(dot(rows(s, split(r)), s, NN))
        power = [o[:T] for o in out]
        result = [r + o[T:] for r, o in zip(result, out)]
    result = [r + dot(split(r), split(p), NN) for r, p in zip(result, power)]
    for size in (32, 64, 128):
        pick = same(size) & ~same(size // 2)
        parts = [split(r) for r in result]
        half = [dot(split(jnp.where(pick, c, 0.0)), s, NN) for c, s in zip(coupling, parts)]
        result = [r - dot(s, split(h), NN) for r, s, h in zip(result, parts, half)]
    return result


def maps_kernel(
    heads,
    q_ref, k_ref, v_ref, halo_ref, gate_ref, beta_ref, conv_ref, decay_ref, grad_ref,
    maps_ref, q_out, k_out, fq_out, fk_out, fv_out, cum_out, gf_out, ld_out, w_out, u_out, pg_out, inv_out,
    ext,
):
    row, col = iota((T, T), 0), iota((T, T), 1)
    strict = row > col
    lower = row >= col
    ident = jnp.where(row == col, 1.0, 0.0)
    tri = jnp.where(lower, 1.0, 0.0).astype(BF16)
    base = pl.program_id(0) * heads
    each = range(heads)
    at = [slice(h * T, (h + 1) * T) for h in each]
    cumul, qs, ks, vs, betas = [], [], [], [], []
    for h in each:
        gate = gate_ref[:, at[h]]
        speed = -jnp.exp(decay_ref[:, at[h]])
        log_decay = speed * (jnp.maximum(gate, 0.0) + jnp.log1p(jnp.exp(-jnp.abs(gate))))
        ld_out[:, at[h]] = log_decay
        gf_out[:, at[h]] = speed * sigmoid(gate)
        both = lax.dot_general(
            tri, jnp.concatenate(split(log_decay), axis=1), NN, preferred_element_type=F32
        )
        cumul.append(both[:, :T] + both[:, T:])
        cum_out[:, at[h]] = cumul[h]
        betas.append(column(beta_ref, base + h))
        acts = []
        for j, (raw, factor) in enumerate(((q_ref, fq_out), (k_ref, fk_out), (v_ref, fv_out))):
            ext[j, h, 5:8] = halo_ref[:, at[h]].astype(F32)[3 * j : 3 * j + 3]
            ext[j, h, 8:136] = raw[:, at[h]].astype(F32)
            pre = conv_ref[j, 0:1, at[h]] * ext[j, h, 5 : 5 + T]
            for i in range(1, 4):
                pre = pre + conv_ref[j, i : i + 1, at[h]] * ext[j, h, 5 + i : 5 + i + T]
            s = sigmoid(pre)
            act = pre * s
            slope = s * (1.0 + pre * (1.0 - s))
            if j < 2:
                scale = lax.rsqrt(jnp.sum(act * act, axis=1, keepdims=True) + EPS)
                act = act * scale
                slope = slope * scale
            factor[:, at[h]] = slope
            acts.append(act)
        qs.append(acts[0])
        ks.append(acts[1])
        vs.append(acts[2])
        q_out[:, at[h]] = acts[0]
        k_out[:, at[h]] = acts[1]
    factors = [gate_factors(c) for c in cumul]
    couple, attend = [], []
    for h in each:
        up0, up1, down, full, end, last, late = factors[h]
        kd = ks[h] * down
        right = lanes(split(jnp.where(late, 0.0, kd)), split(jnp.where(late, kd, 0.0)))
        left = rows(
            lanes(split(ks[h] * up0), split(ks[h] * up1)), lanes(split(qs[h] * up0), split(qs[h] * up1))
        )
        both = dot(left, right, NT)
        couple.append(jnp.where(strict, both[:T], 0.0) * betas[h])
        attend.append(jnp.where(lower, both[T:], 0.0))
    inverse = unit_inverse(couple)
    for h in each:
        up0, up1, down, full, end, last, late = factors[h]
        inv_out[h] = inverse[h]
        both = dot(
            split(inverse[h]), lanes(split(betas[h] * ks[h] * full), split(betas[h] * vs[h])), NN
        )
        w, u = both[:, :T], both[:, T:]
        w_out[h] = w
        u_out[h] = u
        both = dot(split(ks[h] * end), split(both), TN)
        grad = (grad_ref[:, at[h]],)
        pg = dot(split(attend[h]), grad, TN)
        pg_out[h] = pg
        adjoint = dot(split(qs[h] * full), grad, TN) - dot(split(w), split(pg), TN)
        put(maps_ref.at[h], (-both[:, :T], both[:, T:], adjoint), cumul[h][T - 1 : T])


def put(ref, parts, log_decay):
    row = iota((AUX, T), 0)
    packed = jnp.zeros((AUX, T), F32)
    place = 0
    for i, square in enumerate(parts):
        largest = jnp.max(jnp.max(jnp.abs(square), axis=0, keepdims=True), axis=1, keepdims=True)
        power = jnp.floor(jnp.log2(jnp.maximum(largest, 1e-30)))
        ref[place : place + T] = square * jnp.exp2(TOP - power)
        packed = jnp.where(row == 3 + i, power, packed)
        place += T
    if log_decay is not None:
        rest = jnp.maximum(log_decay, FLOOR)
        for i in range(3):
            term = rest.astype(BF16).astype(F32)
            rest = rest - term
            packed = jnp.where(row == i, term, packed)
    ref[place : place + AUX] = packed


def get(ref):
    count = (ref.shape[0] - AUX) // T
    aux = ref[count * T : count * T + AUX]
    squares = [ref[m * T : (m + 1) * T] * jnp.exp2(aux[3 + m : 4 + m] - TOP) for m in range(count)]
    return (*squares, (aux[0:1] + aux[1:2]) + aux[2:3])


def whole_map(move, log_decay):
    row, col = iota((T, T), 0), iota((T, T), 1)
    return move + jnp.where(row == col, jnp.exp(log_decay), 0.0)


def join(early, late):
    ee, eb, ed, eg = early
    le, lb, ld, lg = late
    both = dot(split(whole_map(le, lg)), lanes(split(ee), split(eb)), NN)
    adjoint = ed + dot(split(whole_map(ee, eg)), split(ld), TN)
    return (both[:, :T] + le * jnp.exp(eg), both[:, T:] + lb, adjoint, eg + lg)


def tree(items):
    while len(items) > 1:
        items = [join(items[i], items[i + 1]) for i in range(0, len(items), 2)]
    return items[0]


def line_kernel(maps_ref, out_ref):
    *squares, log_decay = tree([get(maps_ref.at[i]) for i in range(maps_ref.shape[0])])
    put(out_ref, squares, log_decay)


def plane_kernel(where_ref, *refs):
    *lines, one, two, three, held = refs
    count = len(lines)
    mine, plane = where_ref[1], where_ref[0]
    for d, line in enumerate(lines):
        held[lax.rem(mine - d + count, count)] = line[...]
    move, offset, adjoint, log_decay = tree([get(held.at[i]) for i in range(count)])
    for d, out in enumerate((one, two, three)):
        put(out, (move, jnp.where(plane + d + 1 < count, offset, adjoint)), log_decay)


def advance(part, state, active):
    move, offset, log_decay = part
    new = dot(split(whole_map(move, log_decay)), split(state), NN) + offset
    return new if active is None else jnp.where(active, new, state)


def retreat(part, grad, active):
    move, adjoint, log_decay = part
    new = dot(split(whole_map(move, log_decay)), split(grad), TN) + adjoint
    return new if active is None else jnp.where(active, new, grad)


def states_kernel(where_ref, maps_ref, *refs):
    *moved, out_ref = refs
    lines, planes = moved[:3], moved[3:]
    state = jnp.zeros((T, T), F32)
    grad = jnp.zeros((T, T), F32)
    for refs, mine in ((planes, where_ref[0]), (lines, where_ref[1])):
        parts = [get(ref) for ref in refs]
        for i in range(3):
            part = parts[2 - i]
            state = advance((part[0], part[1], part[-1]), state, mine >= 3 - i)
            part = parts[i]
            grad = retreat((part[0], part[-2], part[-1]), grad, mine < i + 1)
    count = maps_ref.shape[0]
    states, grads = [state], [grad]
    for i in range(count - 1):
        move, offset, adjoint, log_decay = get(maps_ref.at[i])
        states.append(advance((move, offset, log_decay), states[-1], None))
        move, offset, adjoint, log_decay = get(maps_ref.at[count - 1 - i])
        grads.append(retreat((move, adjoint, log_decay), grads[-1], None))
    for i in range(count):
        put(out_ref.at[i], (states[i], grads[count - 1 - i]), None)


def grads_kernel(
    heads,
    q_ref, k_ref, v_ref, halo_ref, beta_ref, conv_ref, grad_ref, states_ref,
    q_in, k_in, fq_in, fk_in, fv_in, cum_in, gf_in, ld_in, w_in, u_in, pg_in, inv_in,
    dq_out, dk_out, dv_out, edge_out, tail_out, dgate_out, dbeta_out, params,
    ext, back, tail,
):
    row, col = iota((T, T), 0), iota((T, T), 1)
    strict = row > col
    lower = row >= col
    upper = jnp.where(row <= col, 1.0, 0.0).astype(BF16)
    ones = jnp.ones((8, T), BF16)
    tail[9:16] = jnp.zeros((7, T), F32)
    base = pl.program_id(0) * heads
    each = range(heads)
    at = [slice(h * T, (h + 1) * T) for h in each]
    deltas, dds, grads = [], [], []
    betas = [column(beta_ref, base + h) for h in each]
    factors = [gate_factors(cum_in[:, at[h]]) for h in each]
    states = [get(states_ref.at[h]) for h in each]
    ms = [split(states[h][0]) for h in each]
    gs = [split(states[h][1]) for h in each]
    qs = [q_in[:, at[h]] for h in each]
    ks = [k_in[:, at[h]] for h in each]
    for h in each:
        params[h, 13:16] = jnp.zeros((3, T), F32)
    for h in each:
        deltas.append(u_in[h] - dot(split(w_in[h]), ms[h], NN))
        dds.append(pg_in[h] + dot(split(ks[h] * factors[h][4]), gs[h], NN))
    des = [dot(split(inv_in[h]), split(dds[h]), TN) for h in each]
    dvs = [betas[h] * des[h] for h in each]
    dsp = [split(deltas[h]) for h in each]
    firsts = []
    for h in each:
        grad = grad_ref[:, at[h]]
        left = rows((grad, jnp.zeros_like(grad)), split(-dvs[h]))
        both = [dot(left, dsp[h], NT), dot(left, ms[h], NT)]
        firsts.append(jnp.concatenate(both, axis=1))
    ends = [dot(dsp[h], gs[h], NT) for h in each]
    for h in each:
        up0, up1, down, full, end, last, late = factors[h]
        q, k = qs[h], ks[h]
        first = firsts[h]
        sp = split(jnp.where(lower, first[:T, :T], 0.0))
        sl = split(jnp.where(strict, first[T:, :T], 0.0))
        kd = k * down
        right = lanes(split(jnp.where(late, 0.0, kd)), split(jnp.where(late, kd, 0.0)))
        by_row = dot(rows(sp, sl), right, NN)
        up = rows(lanes(split(k * up0), split(k * up1)), lanes(split(q * up0), split(q * up1)))
        by_col = dot(rows(sl, sp), up, TN)
        dq = full * first[:T, T:] + up0 * by_row[:T, :T] + up1 * by_row[:T, T:]
        dk_row = full * first[T:, T:] + up0 * by_row[T:, :T] + up1 * by_row[T:, T:]
        dk_end = end * ends[h]
        dk_col = down * jnp.where(late, by_col[:, T:], by_col[:, :T]) + dk_end
        dk = dk_row + dk_col
        dcum = q * dq + k * (dk_row - dk_col)
        held = states[h][0] * states[h][1]
        dlast = jnp.sum(k * dk_end, axis=0, keepdims=True) + last * dot((ones,), split(held), NT)[0:1]
        both = lax.dot_general(
            upper, jnp.concatenate(split(dcum), axis=1), NN, preferred_element_type=F32
        )
        dlog = both[:, :T] + both[:, T:] + dlast
        dgate_out[:, at[h]] = dlog * gf_in[:, at[h]]
        params[h, 12:13] = jnp.sum(dlog * ld_in[:, at[h]], axis=0, keepdims=True)
        write = jnp.sum(des[h] * deltas[h], axis=1, keepdims=True) * (1.0 - betas[h])
        dbeta_out[pl.ds(base + h, 1)] = jnp.sum(jnp.where(row == col, write, 0.0), axis=0, keepdims=True)
        pres = (
            fq_in[:, at[h]] * (dq - q * jnp.sum(q * dq, axis=1, keepdims=True)),
            fk_in[:, at[h]] * (dk - k * jnp.sum(k * dk, axis=1, keepdims=True)),
            fv_in[:, at[h]] * dvs[h],
        )
        for j, (raw, out) in enumerate(((q_ref, dq_out), (k_ref, dk_out), (v_ref, dv_out))):
            ext[j, h, 5:8] = halo_ref[:, at[h]].astype(F32)[3 * j : 3 * j + 3]
            ext[j, h, 8:136] = raw[:, at[h]].astype(F32)
            back[j, h, 0:8] = jnp.zeros((8, T), F32)
            back[j, h, 8:136] = pres[j]
            back[j, h, 136:144] = jnp.zeros((8, T), F32)
            whole = None
            for i in range(4):
                part = conv_ref[j, i : i + 1, at[h]] * back[j, h, 3 - i : 3 - i + 136]
                whole = part if whole is None else whole + part
                params[h, 4 * j + i : 4 * j + i + 1] = jnp.sum(
                    pres[j] * ext[j, h, 5 + i : 5 + i + T], axis=0, keepdims=True
                )
            out[:, at[h]] = whole[8:136].astype(BF16)
            tail[3 * j : 3 * j + 3] = whole[5:8]
            edge_out[j, :, at[h]] = whole[120:136]
        tail_out[:, at[h]] = tail[...].astype(BF16)


def ends_kernel(q_ref, k_ref, v_ref, out_ref):
    row = iota(out_ref.shape, 0)
    packed = jnp.zeros(out_ref.shape, F32)
    for j, ref in enumerate((q_ref, k_ref, v_ref)):
        turned = pltpu.roll(ref[...].astype(F32), 3 * j + 3, axis=0)
        packed = jnp.where((row >= 3 * j) & (row < 3 * j + 3), turned, packed)
    out_ref[...] = packed.astype(BF16)


def share_kernel(parts_ref, out_ref):
    total = parts_ref[0]
    for i in range(1, parts_ref.shape[0]):
        total = total + parts_ref[i]
    for i in range(out_ref.shape[0]):
        out_ref[i] = total


def gather_kernel(parts_ref, conv_out, decay_out):
    for h in range(parts_ref.shape[0]):
        lane = slice(h * T, (h + 1) * T)
        for j in range(3):
            conv_out[j, :, lane] = parts_ref[h, 4 * j : 4 * j + 4]
        decay_out[:, lane] = parts_ref[h, 12:13]


def widen(x):
    return x.astype(F32)


def per_device(query_raw, key_raw, value_raw, gate_raw, beta_raw, conv_weight, decay_log, grad_out):
    length, channels = gate_raw.shape
    count = beta_raw.shape[1]
    lines, planes = lax.axis_size("x"), lax.axis_size("y")
    depth = lax.axis_size("z")
    devices = lines * planes * depth
    wheres = jnp.stack([lax.axis_index("y"), lax.axis_index("x")]).astype(jnp.int32)
    ends = pl.pallas_call(
        ends_kernel, grid=(1,), out_shape=jax.ShapeDtypeStruct((16, channels), BF16),
        in_specs=[pl.BlockSpec((16, channels), lambda i: (length // 16 - 1, 0))] * 3,
        out_specs=pl.BlockSpec((16, channels), lambda i: (0, 0)), name="last_rows",
        compiler_params=pltpu.CompilerParams(vmem_limit_bytes=60 * MIB),
    )(query_raw, key_raw, value_raw)
    halo = lax.ppermute(ends, SEQ, [(i, i + 1) for i in range(devices - 1)])
    decay_row = decay_log.reshape(1, channels)

    def specs(heads):
        wide = heads * T
        return (
            pl.BlockSpec((T, wide), lambda h: (0, h)),
            pl.BlockSpec((16, wide), lambda h: (0, h)),
            pl.BlockSpec((3, 4, wide), lambda h: (0, 0, h)),
            pl.BlockSpec((count, T), lambda h: (0, 0)),
            pl.BlockSpec((heads, T, T), lambda h: (h, 0, 0)),
        )

    def like(*shape, dtype=F32):
        return jax.ShapeDtypeStruct(shape, dtype)

    params = pltpu.CompilerParams(
        dimension_semantics=("arbitrary",), vmem_limit_bytes=60 * MIB
    )
    saved_shapes = [like(length, channels)] * 8 + [like(count, T, T)] * 4
    heads = MAPS_GROUP
    wide = heads * T
    tall, edge, taps, beta_spec, square = specs(heads)
    saved_specs = [tall] * 8 + [square] * 4
    maps, *saved = pl.pallas_call(
        functools.partial(maps_kernel, heads),
        grid=(count // heads,),
        in_specs=[tall, tall, tall, edge, tall, beta_spec, taps, pl.BlockSpec((1, wide), lambda h: (0, h)), tall],
        out_specs=[pl.BlockSpec((heads, 3 * T + AUX, T), lambda h: (h, 0, 0))] + saved_specs,
        out_shape=[like(count, 3 * T + AUX, T)] + saved_shapes,
        scratch_shapes=[pltpu.VMEM((3, heads, 136, T), F32)],
        compiler_params=params,
        name="block_maps",
    )(query_raw, key_raw, value_raw, halo, gate_raw, beta_raw.T, conv_weight, decay_row, grad_out)

    line_maps = widen(lax.all_to_all(maps.astype(LINK), "z", 0, 0, tiled=True))
    small = pltpu.CompilerParams(vmem_limit_bytes=32 * MIB)
    line_total = pl.pallas_call(
        line_kernel, out_shape=like(3 * T + AUX, T), name="line_total", compiler_params=small
    )(line_maps)

    def around(blocks, axis):
        size = lax.axis_size(axis)
        return [
            lax.ppermute(block, axis, [(i, (i + d + 1) % size) for i in range(size)])
            for d, block in enumerate(blocks)
        ]

    smem = pl.BlockSpec(memory_space=pltpu.SMEM)
    vmem = pl.BlockSpec(memory_space=pltpu.VMEM)
    from_lines = [widen(x) for x in around([line_total.astype(LINK)] * 3, "x")]
    plane_totals = pl.pallas_call(
        plane_kernel, out_shape=[like(2 * T + AUX, T)] * 3, in_specs=[smem] + [vmem] * 4,
        scratch_shapes=[pltpu.VMEM((4, 3 * T + AUX, T), F32)], name="plane_total", compiler_params=small,
    )(wheres, line_total, *from_lines)
    from_planes = [widen(x) for x in around([x.astype(LINK) for x in plane_totals], "y")]
    line_states = pl.pallas_call(
        states_kernel, out_shape=like(depth, 2 * T + AUX, T), in_specs=[smem] + [vmem] * 7,
        name="line_states", compiler_params=small,
    )(wheres, line_maps, *from_lines, *from_planes)
    states = widen(lax.all_to_all(line_states.astype(LINK), "z", 0, 0, tiled=True))

    heads = GRADS_GROUP
    wide = heads * T
    tall, edge, taps, beta_spec, square = specs(heads)
    saved_specs = [tall] * 8 + [square] * 4
    dq, dk, dv, edges, tails, dgate, dbeta, sums = pl.pallas_call(
        functools.partial(grads_kernel, heads),
        grid=(count // heads,),
        in_specs=[
            tall, tall, tall, edge, beta_spec, taps, tall,
            pl.BlockSpec((heads, 2 * T + AUX, T), lambda h: (h, 0, 0)),
        ] + saved_specs,
        out_specs=[
            tall, tall, tall,
            pl.BlockSpec((3, 16, wide), lambda h: (0, 0, h)), edge, tall, beta_spec,
            pl.BlockSpec((heads, 16, T), lambda h: (h, 0, 0)),
        ],
        out_shape=[like(length, channels, dtype=BF16)] * 3
        + [like(3, 16, channels), like(16, channels, dtype=BF16), like(length, channels), like(count, length), like(count, 16, T)],
        scratch_shapes=[pltpu.VMEM((3, heads, 136, T), F32), pltpu.VMEM((3, heads, 144, T), F32), pltpu.VMEM((16, T), F32)],
        compiler_params=pltpu.CompilerParams(
            dimension_semantics=("arbitrary",), vmem_limit_bytes=26 * MIB
        ),
        name="block_grads",
    )(query_raw, key_raw, value_raw, halo, beta_raw.T, conv_weight, grad_out, states, *saved)

    after = lax.ppermute(tails, SEQ, [(i + 1, i) for i in range(devices - 1)])
    def finish(full, extra):
        return lax.dynamic_update_slice(full, extra.astype(BF16), (length - 16, 0))


    def share(parts, copies):
        return pl.pallas_call(
            share_kernel, out_shape=like(copies, 16, T), name="share_sums", compiler_params=small
        )(parts)

    across = ("y", "x")
    sums = share(lax.all_to_all(sums, "z", 0, 0, tiled=True), lines * planes)
    sums = share(lax.all_to_all(sums, across, 0, 0, tiled=True), depth)
    sums, after = lax.optimization_barrier((sums, after))
    fixed = edges + jnp.pad(after[:9].astype(F32).reshape(3, 3, channels), ((0, 0), (13, 0), (0, 0)))

    conv_sum, decay_sum = pl.pallas_call(
        gather_kernel, out_shape=[like(3, 4, channels), like(1, channels)],
        name="gather_sums", compiler_params=small,
    )(lax.all_to_all(sums, "z", 0, 0, tiled=True))
    return (
        finish(dq, fixed[0]),
        finish(dk, fixed[1]),
        finish(dv, fixed[2]),
        dgate,
        dbeta.T,
        conv_sum,
        decay_sum.reshape(channels),
    )


MAPS_GROUP = 8
GRADS_GROUP = 4


def solution(mesh):
    inner = Mesh(mesh.devices.reshape(4, 4, 8, 2), SEQ + ("head",))
    wide = P(SEQ, "head")
    in_specs = (wide, wide, wide, wide, wide, P(None, None, "head"), P("head"), wide)
    out_specs = (wide, wide, wide, wide, wide, P(None, None, "head"), P("head"))
    return jax.shard_map(
        per_device, mesh=inner, in_specs=in_specs, out_specs=out_specs, check_vma=False
    )
```

```python
import functools

import jax
import jax.numpy as jnp
from jax import lax
from jax.experimental import pallas as pl
from jax.experimental.pallas import tpu as pltpu
from jax.sharding import Mesh
from jax.sharding import PartitionSpec as P

F32 = jnp.float32
BF16 = jnp.bfloat16
EPS = 1e-06
T = 128
SEQ = ("y", "x", "z")
NN = (((1,), (0,)), ((), ()))
NT = (((1,), (1,)), ((), ()))
TN = (((0,), (0,)), ((), ()))
MIB = 1024 * 1024
AUX = 16
WIDEST = 128
LINK = jnp.float16
TOP = 13.0
FLOOR = -200.0


def split(x):
    hi = x.astype(BF16)
    return (hi, (x - hi.astype(F32)).astype(BF16))


def dot(a, b, dims):
    (left_dim,), (right_dim,) = dims[0]
    width = b[0].shape[1 - right_dim]

    def run(left, right):
        return lax.dot_general(left, right, dims, preferred_element_type=F32)

    if len(a) == 1 and len(b) == 1:
        return run(a[0], b[0])
    if len(b) == 1:
        return run(jnp.concatenate(a, axis=left_dim), jnp.concatenate([b[0]] * 2, axis=right_dim))
    if len(a) == 1:
        both = run(a[0], jnp.concatenate(b, axis=1 - right_dim))
        return both[:, :width] + both[:, width:]
    left = jnp.concatenate(a, axis=left_dim)
    right = jnp.concatenate([b[0]] * 2, axis=right_dim)
    if width > WIDEST:
        return run(left, right) + run(a[0], b[1])
    low = jnp.concatenate([b[1]] * 2, axis=right_dim)
    both = run(left, jnp.concatenate([right, low], axis=1 - right_dim))
    return both[:, :width] + both[:, width:]


def lanes(*parts):
    return tuple(jnp.concatenate(terms, axis=1) for terms in zip(*parts))


def rows(*parts):
    return tuple(jnp.concatenate(terms, axis=0) for terms in zip(*parts))


def iota(shape, dim):
    return lax.broadcasted_iota(jnp.int32, shape, dim)


def sigmoid(x):
    return 1.0 / (1.0 + jnp.exp(-x))


def column(ref, head):
    square = iota((T, T), 0) == iota((T, T), 1)
    return jnp.sum(jnp.where(square, sigmoid(ref[pl.ds(head, 1)]), 0.0), axis=1, keepdims=True)


def gate_factors(cumul):
    row = iota((T, T), 0)
    late = row >= T // 2
    mid0 = cumul[T // 4 : T // 4 + 1]
    mid1 = cumul[3 * T // 4 : 3 * T // 4 + 1]
    last = cumul[T - 1 : T]
    up0 = jnp.exp(cumul - mid0)
    up1 = jnp.where(late, jnp.exp(jnp.where(late, cumul - mid1, 0.0)), 0.0)
    down = jnp.exp(jnp.where(late, mid1, mid0) - cumul)
    return up0, up1, down, jnp.exp(cumul), jnp.exp(last - cumul), jnp.exp(last), late


def unit_inverse(coupling):
    row, col = iota((T, T), 0), iota((T, T), 1)
    ident = jnp.where(row == col, 1.0, 0.0)

    def same(size):
        return (row // size) == (col // size)

    inner = [jnp.where(same(16), c, 0.0) for c in coupling]
    result = [ident - c for c in inner]
    power = []
    for c in inner:
        s = split(c)
        power.append(dot(s, s, NN))
    for level in range(2):
        out = []
        for p, r in zip(power, result):
            s = split(p)
            out.append(dot(rows(s, split(r)), s, NN))
        power = [o[:T] for o in out]
        result = [r + o[T:] for r, o in zip(result, out)]
    result = [r + dot(split(r), split(p), NN) for r, p in zip(result, power)]
    for size in (32, 64, 128):
        pick = same(size) & ~same(size // 2)
        parts = [split(r) for r in result]
        half = [dot(split(jnp.where(pick, c, 0.0)), s, NN) for c, s in zip(coupling, parts)]
        result = [r - dot(s, split(h), NN) for r, s, h in zip(result, parts, half)]
    return result


def decays_kernel(heads, gate_ref, decay_ref, cum_out, gf_out, ld_out):
    tri = jnp.where(iota((T, T), 0) >= iota((T, T), 1), 1.0, 0.0).astype(BF16)
    for h in range(heads):
        lane = slice(h * T, (h + 1) * T)
        gate = gate_ref[:, lane]
        speed = -jnp.exp(decay_ref[:, lane])
        log_decay = speed * (jnp.maximum(gate, 0.0) + jnp.log1p(jnp.exp(-jnp.abs(gate))))
        ld_out[:, lane] = log_decay
        gf_out[:, lane] = speed * sigmoid(gate)
        both = lax.dot_general(
            tri, jnp.concatenate(split(log_decay), axis=1), NN, preferred_element_type=F32
        )
        cum_out[:, lane] = both[:, :T] + both[:, T:]


def maps_kernel(
    heads,
    q_ref, k_ref, v_ref, halo_ref, cum_ref, beta_ref, conv_ref, grad_ref,
    maps_ref, q_out, k_out, fq_out, fk_out, fv_out, w_out, u_out, pg_out, inv_out,
    ext,
):
    row, col = iota((T, T), 0), iota((T, T), 1)
    strict = row > col
    lower = row >= col
    ident = jnp.where(row == col, 1.0, 0.0)
    base = pl.program_id(0) * heads
    each = range(heads)
    at = [slice(h * T, (h + 1) * T) for h in each]
    cumul, qs, ks, vs, betas = [], [], [], [], []
    for h in each:
        cumul.append(cum_ref[:, at[h]])
        betas.append(column(beta_ref, base + h))
        acts = []
        for j, (raw, factor) in enumerate(((q_ref, fq_out), (k_ref, fk_out), (v_ref, fv_out))):
            ext[j, h, 5:8] = halo_ref[:, at[h]].astype(F32)[3 * j : 3 * j + 3]
            ext[j, h, 8:136] = raw[:, at[h]].astype(F32)
            pre = conv_ref[j, 0:1, at[h]] * ext[j, h, 5 : 5 + T]
            for i in range(1, 4):
                pre = pre + conv_ref[j, i : i + 1, at[h]] * ext[j, h, 5 + i : 5 + i + T]
            s = sigmoid(pre)
            act = pre * s
            slope = s * (1.0 + pre * (1.0 - s))
            if j < 2:
                scale = lax.rsqrt(jnp.sum(act * act, axis=1, keepdims=True) + EPS)
                act = act * scale
                slope = slope * scale
            factor[:, at[h]] = slope
            acts.append(act)
        qs.append(acts[0])
        ks.append(acts[1])
        vs.append(acts[2])
        q_out[:, at[h]] = acts[0]
        k_out[:, at[h]] = acts[1]
    factors = [gate_factors(c) for c in cumul]
    couple, attend = [], []
    for h in each:
        up0, up1, down, full, end, last, late = factors[h]
        kd = ks[h] * down
        right = lanes(split(jnp.where(late, 0.0, kd)), split(jnp.where(late, kd, 0.0)))
        left = rows(
            lanes(split(ks[h] * up0), split(ks[h] * up1)), lanes(split(qs[h] * up0), split(qs[h] * up1))
        )
        both = dot(left, right, NT)
        couple.append(jnp.where(strict, both[:T], 0.0) * betas[h])
        attend.append(jnp.where(lower, both[T:], 0.0))
    inverse = unit_inverse(couple)
    for h in each:
        up0, up1, down, full, end, last, late = factors[h]
        inv_out[h] = inverse[h]
        both = dot(
            split(inverse[h]), lanes(split(betas[h] * ks[h] * full), split(betas[h] * vs[h])), NN
        )
        w, u = both[:, :T], both[:, T:]
        w_out[h] = w
        u_out[h] = u
        both = dot(split(ks[h] * end), split(both), TN)
        grad = (grad_ref[:, at[h]],)
        pg = dot(split(attend[h]), grad, TN)
        pg_out[h] = pg
        adjoint = dot(split(qs[h] * full), grad, TN) - dot(split(w), split(pg), TN)
        put(maps_ref.at[h], (-both[:, :T], both[:, T:], adjoint), cumul[h][T - 1 : T])


def put(ref, parts, log_decay):
    row = iota((AUX, T), 0)
    packed = jnp.zeros((AUX, T), F32)
    place = 0
    for i, square in enumerate(parts):
        largest = jnp.max(jnp.max(jnp.abs(square), axis=0, keepdims=True), axis=1, keepdims=True)
        power = jnp.floor(jnp.log2(jnp.maximum(largest, 1e-30)))
        ref[place : place + T] = square * jnp.exp2(TOP - power)
        packed = jnp.where(row == 3 + i, power, packed)
        place += T
    if log_decay is not None:
        rest = jnp.maximum(log_decay, FLOOR)
        for i in range(3):
            term = rest.astype(BF16).astype(F32)
            rest = rest - term
            packed = jnp.where(row == i, term, packed)
    ref[place : place + AUX] = packed


def get(ref):
    count = (ref.shape[0] - AUX) // T
    aux = ref[count * T : count * T + AUX]
    squares = [ref[m * T : (m + 1) * T] * jnp.exp2(aux[3 + m : 4 + m] - TOP) for m in range(count)]
    return (*squares, (aux[0:1] + aux[1:2]) + aux[2:3])


def whole_map(move, log_decay):
    row, col = iota((T, T), 0), iota((T, T), 1)
    return move + jnp.where(row == col, jnp.exp(log_decay), 0.0)


def join(early, late):
    ee, eb, ed, eg = early
    le, lb, ld, lg = late
    both = dot(split(whole_map(le, lg)), lanes(split(ee), split(eb)), NN)
    adjoint = ed + dot(split(whole_map(ee, eg)), split(ld), TN)
    return (both[:, :T] + le * jnp.exp(eg), both[:, T:] + lb, adjoint, eg + lg)


def tree(items):
    while len(items) > 1:
        items = [join(items[i], items[i + 1]) for i in range(0, len(items), 2)]
    return items[0]


def line_kernel(maps_ref, out_ref):
    *squares, log_decay = tree([get(maps_ref.at[i]) for i in range(maps_ref.shape[0])])
    put(out_ref, squares, log_decay)


def plane_kernel(where_ref, *refs):
    *lines, one, two, three, held = refs
    count = len(lines)
    mine, plane = where_ref[1], where_ref[0]
    for d, line in enumerate(lines):
        held[lax.rem(mine - d + count, count)] = line[...]
    move, offset, adjoint, log_decay = tree([get(held.at[i]) for i in range(count)])
    for d, out in enumerate((one, two, three)):
        put(out, (move, jnp.where(plane + d + 1 < count, offset, adjoint)), log_decay)


def advance(part, state, active):
    move, offset, log_decay = part
    new = dot(split(whole_map(move, log_decay)), split(state), NN) + offset
    return new if active is None else jnp.where(active, new, state)


def retreat(part, grad, active):
    move, adjoint, log_decay = part
    new = dot(split(whole_map(move, log_decay)), split(grad), TN) + adjoint
    return new if active is None else jnp.where(active, new, grad)


def states_kernel(where_ref, maps_ref, *refs):
    *moved, out_ref = refs
    lines, planes = moved[:3], moved[3:]
    state = jnp.zeros((T, T), F32)
    grad = jnp.zeros((T, T), F32)
    for refs, mine in ((planes, where_ref[0]), (lines, where_ref[1])):
        parts = [get(ref) for ref in refs]
        for i in range(3):
            part = parts[2 - i]
            state = advance((part[0], part[1], part[-1]), state, mine >= 3 - i)
            part = parts[i]
            grad = retreat((part[0], part[-2], part[-1]), grad, mine < i + 1)
    count = maps_ref.shape[0]
    states, grads = [state], [grad]
    for i in range(count - 1):
        move, offset, adjoint, log_decay = get(maps_ref.at[i])
        states.append(advance((move, offset, log_decay), states[-1], None))
        move, offset, adjoint, log_decay = get(maps_ref.at[count - 1 - i])
        grads.append(retreat((move, adjoint, log_decay), grads[-1], None))
    for i in range(count):
        put(out_ref.at[i], (states[i], grads[count - 1 - i]), None)


def grads_kernel(
    heads,
    q_ref, k_ref, v_ref, halo_ref, beta_ref, conv_ref, grad_ref, states_ref,
    q_in, k_in, fq_in, fk_in, fv_in, cum_in, gf_in, ld_in, w_in, u_in, pg_in, inv_in,
    dq_out, dk_out, dv_out, edge_out, tail_out, dgate_out, dbeta_out, params,
    ext, back, tail,
):
    row, col = iota((T, T), 0), iota((T, T), 1)
    strict = row > col
    lower = row >= col
    upper = jnp.where(row <= col, 1.0, 0.0).astype(BF16)
    ones = jnp.ones((8, T), BF16)
    tail[9:16] = jnp.zeros((7, T), F32)
    base = pl.program_id(0) * heads
    each = range(heads)
    at = [slice(h * T, (h + 1) * T) for h in each]
    deltas, dds, grads = [], [], []
    betas = [column(beta_ref, base + h) for h in each]
    factors = [gate_factors(cum_in[:, at[h]]) for h in each]
    states = [get(states_ref.at[h]) for h in each]
    ms = [split(states[h][0]) for h in each]
    gs = [split(states[h][1]) for h in each]
    qs = [q_in[:, at[h]] for h in each]
    ks = [k_in[:, at[h]] for h in each]
    for h in each:
        params[h, 13:16] = jnp.zeros((3, T), F32)
    for h in each:
        deltas.append(u_in[h] - dot(split(w_in[h]), ms[h], NN))
        dds.append(pg_in[h] + dot(split(ks[h] * factors[h][4]), gs[h], NN))
    des = [dot(split(inv_in[h]), split(dds[h]), TN) for h in each]
    dvs = [betas[h] * des[h] for h in each]
    dsp = [split(deltas[h]) for h in each]
    firsts = []
    for h in each:
        grad = grad_ref[:, at[h]]
        left = rows((grad, jnp.zeros_like(grad)), split(-dvs[h]))
        both = [dot(left, dsp[h], NT), dot(left, ms[h], NT)]
        firsts.append(jnp.concatenate(both, axis=1))
    ends = [dot(dsp[h], gs[h], NT) for h in each]
    for h in each:
        up0, up1, down, full, end, last, late = factors[h]
        q, k = qs[h], ks[h]
        first = firsts[h]
        sp = split(jnp.where(lower, first[:T, :T], 0.0))
        sl = split(jnp.where(strict, first[T:, :T], 0.0))
        kd = k * down
        right = lanes(split(jnp.where(late, 0.0, kd)), split(jnp.where(late, kd, 0.0)))
        by_row = dot(rows(sp, sl), right, NN)
        up = rows(lanes(split(k * up0), split(k * up1)), lanes(split(q * up0), split(q * up1)))
        by_col = dot(rows(sl, sp), up, TN)
        dq = full * first[:T, T:] + up0 * by_row[:T, :T] + up1 * by_row[:T, T:]
        dk_row = full * first[T:, T:] + up0 * by_row[T:, :T] + up1 * by_row[T:, T:]
        dk_end = end * ends[h]
        dk_col = down * jnp.where(late, by_col[:, T:], by_col[:, :T]) + dk_end
        dk = dk_row + dk_col
        dcum = q * dq + k * (dk_row - dk_col)
        held = states[h][0] * states[h][1]
        dlast = jnp.sum(k * dk_end, axis=0, keepdims=True) + last * dot((ones,), split(held), NT)[0:1]
        both = lax.dot_general(
            upper, jnp.concatenate(split(dcum), axis=1), NN, preferred_element_type=F32
        )
        dlog = both[:, :T] + both[:, T:] + dlast
        dgate_out[:, at[h]] = dlog * gf_in[:, at[h]]
        params[h, 12:13] = jnp.sum(dlog * ld_in[:, at[h]], axis=0, keepdims=True)
        write = jnp.sum(des[h] * deltas[h], axis=1, keepdims=True) * (1.0 - betas[h])
        dbeta_out[pl.ds(base + h, 1)] = jnp.sum(jnp.where(row == col, write, 0.0), axis=0, keepdims=True)
        pres = (
            fq_in[:, at[h]] * (dq - q * jnp.sum(q * dq, axis=1, keepdims=True)),
            fk_in[:, at[h]] * (dk - k * jnp.sum(k * dk, axis=1, keepdims=True)),
            fv_in[:, at[h]] * dvs[h],
        )
        for j, (raw, out) in enumerate(((q_ref, dq_out), (k_ref, dk_out), (v_ref, dv_out))):
            ext[j, h, 5:8] = halo_ref[:, at[h]].astype(F32)[3 * j : 3 * j + 3]
            ext[j, h, 8:136] = raw[:, at[h]].astype(F32)
            back[j, h, 0:8] = jnp.zeros((8, T), F32)
            back[j, h, 8:136] = pres[j]
            back[j, h, 136:144] = jnp.zeros((8, T), F32)
            whole = None
            for i in range(4):
                part = conv_ref[j, i : i + 1, at[h]] * back[j, h, 3 - i : 3 - i + 136]
                whole = part if whole is None else whole + part
                params[h, 4 * j + i : 4 * j + i + 1] = jnp.sum(
                    pres[j] * ext[j, h, 5 + i : 5 + i + T], axis=0, keepdims=True
                )
            out[:, at[h]] = whole[8:136].astype(BF16)
            tail[3 * j : 3 * j + 3] = whole[5:8]
            edge_out[j, :, at[h]] = whole[120:136]
        tail_out[:, at[h]] = tail[...].astype(BF16)


def ends_kernel(q_ref, k_ref, v_ref, out_ref):
    row = iota(out_ref.shape, 0)
    packed = jnp.zeros(out_ref.shape, F32)
    for j, ref in enumerate((q_ref, k_ref, v_ref)):
        turned = pltpu.roll(ref[...].astype(F32), 3 * j + 3, axis=0)
        packed = jnp.where((row >= 3 * j) & (row < 3 * j + 3), turned, packed)
    out_ref[...] = packed.astype(BF16)


def share_kernel(parts_ref, out_ref):
    total = parts_ref[0]
    for i in range(1, parts_ref.shape[0]):
        total = total + parts_ref[i]
    for i in range(out_ref.shape[0]):
        out_ref[i] = total


def gather_kernel(parts_ref, conv_out, decay_out):
    for h in range(parts_ref.shape[0]):
        lane = slice(h * T, (h + 1) * T)
        for j in range(3):
            conv_out[j, :, lane] = parts_ref[h, 4 * j : 4 * j + 4]
        decay_out[:, lane] = parts_ref[h, 12:13]


def widen(x):
    return x.astype(F32)


def per_device(query_raw, key_raw, value_raw, gate_raw, beta_raw, conv_weight, decay_log, grad_out):
    length, channels = gate_raw.shape
    count = beta_raw.shape[1]
    lines, planes = lax.axis_size("x"), lax.axis_size("y")
    depth = lax.axis_size("z")
    devices = lines * planes * depth
    wheres = jnp.stack([lax.axis_index("y"), lax.axis_index("x")]).astype(jnp.int32)
    ends = pl.pallas_call(
        ends_kernel, grid=(1,), out_shape=jax.ShapeDtypeStruct((16, channels), BF16),
        in_specs=[pl.BlockSpec((16, channels), lambda i: (length // 16 - 1, 0))] * 3,
        out_specs=pl.BlockSpec((16, channels), lambda i: (0, 0)), name="last_rows",
        compiler_params=pltpu.CompilerParams(vmem_limit_bytes=60 * MIB),
    )(query_raw, key_raw, value_raw)
    halo = lax.ppermute(ends, SEQ, [(i, i + 1) for i in range(devices - 1)])
    decay_row = decay_log.reshape(1, channels)

    def specs(heads):
        wide = heads * T
        return (
            pl.BlockSpec((T, wide), lambda h: (0, h)),
            pl.BlockSpec((16, wide), lambda h: (0, h)),
            pl.BlockSpec((3, 4, wide), lambda h: (0, 0, h)),
            pl.BlockSpec((count, T), lambda h: (0, 0)),
            pl.BlockSpec((heads, T, T), lambda h: (h, 0, 0)),
        )

    def like(*shape, dtype=F32):
        return jax.ShapeDtypeStruct(shape, dtype)

    params = pltpu.CompilerParams(
        dimension_semantics=("arbitrary",), vmem_limit_bytes=60 * MIB
    )
    saved_shapes = [like(length, channels)] * 8 + [like(count, T, T)] * 4
    heads = MAPS_GROUP
    wide = heads * T
    tall, edge, taps, beta_spec, square = specs(heads)
    saved_specs = [tall] * 8 + [square] * 4
    half = 4 * T
    narrow = pl.BlockSpec((length, half), lambda h: (0, h))
    cumul, slope, log_decay = pl.pallas_call(
        functools.partial(decays_kernel, 4),
        grid=(channels // half,),
        in_specs=[narrow, pl.BlockSpec((1, half), lambda h: (0, h))],
        out_specs=[narrow] * 3,
        out_shape=[like(length, channels)] * 3,
        compiler_params=params,
        name="block_decays",
        cost_estimate=pl.CostEstimate(flops=80_000_000, bytes_accessed=2_500_000, transcendentals=500_000),
    )(gate_raw, decay_row)
    maps, *saved = pl.pallas_call(
        functools.partial(maps_kernel, heads),
        grid=(count // heads,),
        in_specs=[tall, tall, tall, edge, tall, beta_spec, taps, tall],
        out_specs=[pl.BlockSpec((heads, 3 * T + AUX, T), lambda h: (h, 0, 0))] + [tall] * 5 + [square] * 4,
        out_shape=[like(count, 3 * T + AUX, T)] + [like(length, channels)] * 5 + [like(count, T, T)] * 4,
        scratch_shapes=[pltpu.VMEM((3, heads, 136, T), F32)],
        compiler_params=params,
        name="block_maps",
    )(query_raw, key_raw, value_raw, halo, cumul, beta_raw.T, conv_weight, grad_out)
    saved = [*saved[:5], cumul, slope, log_decay, *saved[5:]]

    line_maps = widen(lax.all_to_all(maps.astype(LINK), "z", 0, 0, tiled=True))
    small = pltpu.CompilerParams(vmem_limit_bytes=32 * MIB)
    line_total = pl.pallas_call(
        line_kernel, out_shape=like(3 * T + AUX, T), name="line_total", compiler_params=small
    )(line_maps)

    def around(blocks, axis):
        size = lax.axis_size(axis)
        return [
            lax.ppermute(block, axis, [(i, (i + d + 1) % size) for i in range(size)])
            for d, block in enumerate(blocks)
        ]

    smem = pl.BlockSpec(memory_space=pltpu.SMEM)
    vmem = pl.BlockSpec(memory_space=pltpu.VMEM)
    from_lines = [widen(x) for x in around([line_total.astype(LINK)] * 3, "x")]
    plane_totals = pl.pallas_call(
        plane_kernel, out_shape=[like(2 * T + AUX, T)] * 3, in_specs=[smem] + [vmem] * 4,
        scratch_shapes=[pltpu.VMEM((4, 3 * T + AUX, T), F32)], name="plane_total", compiler_params=small,
    )(wheres, line_total, *from_lines)
    from_planes = [widen(x) for x in around([x.astype(LINK) for x in plane_totals], "y")]
    line_states = pl.pallas_call(
        states_kernel, out_shape=like(depth, 2 * T + AUX, T), in_specs=[smem] + [vmem] * 7,
        name="line_states", compiler_params=small,
    )(wheres, line_maps, *from_lines, *from_planes)
    states = widen(lax.all_to_all(line_states.astype(LINK), "z", 0, 0, tiled=True))

    heads = GRADS_GROUP
    wide = heads * T
    tall, edge, taps, beta_spec, square = specs(heads)
    saved_specs = [tall] * 8 + [square] * 4
    dq, dk, dv, edges, tails, dgate, dbeta, sums = pl.pallas_call(
        functools.partial(grads_kernel, heads),
        grid=(count // heads,),
        in_specs=[
            tall, tall, tall, edge, beta_spec, taps, tall,
            pl.BlockSpec((heads, 2 * T + AUX, T), lambda h: (h, 0, 0)),
        ] + saved_specs,
        out_specs=[
            tall, tall, tall,
            pl.BlockSpec((3, 16, wide), lambda h: (0, 0, h)), edge, tall, beta_spec,
            pl.BlockSpec((heads, 16, T), lambda h: (h, 0, 0)),
        ],
        out_shape=[like(length, channels, dtype=BF16)] * 3
        + [like(3, 16, channels), like(16, channels, dtype=BF16), like(length, channels), like(count, length), like(count, 16, T)],
        scratch_shapes=[pltpu.VMEM((3, heads, 136, T), F32), pltpu.VMEM((3, heads, 144, T), F32), pltpu.VMEM((16, T), F32)],
        compiler_params=pltpu.CompilerParams(
            dimension_semantics=("arbitrary",), vmem_limit_bytes=26 * MIB
        ),
        name="block_grads",
    )(query_raw, key_raw, value_raw, halo, beta_raw.T, conv_weight, grad_out, states, *saved)

    after = lax.ppermute(tails, SEQ, [(i + 1, i) for i in range(devices - 1)])
    def finish(full, extra):
        return lax.dynamic_update_slice(full, extra.astype(BF16), (length - 16, 0))


    def share(parts, copies):
        return pl.pallas_call(
            share_kernel, out_shape=like(copies, 16, T), name="share_sums", compiler_params=small
        )(parts)

    across = ("y", "x")
    sums = share(lax.all_to_all(sums, "z", 0, 0, tiled=True), lines * planes)
    sums = share(lax.all_to_all(sums, across, 0, 0, tiled=True), depth)
    sums, after = lax.optimization_barrier((sums, after))
    fixed = edges + jnp.pad(after[:9].astype(F32).reshape(3, 3, channels), ((0, 0), (13, 0), (0, 0)))

    conv_sum, decay_sum = pl.pallas_call(
        gather_kernel, out_shape=[like(3, 4, channels), like(1, channels)],
        name="gather_sums", compiler_params=small,
    )(lax.all_to_all(sums, "z", 0, 0, tiled=True))
    return (
        finish(dq, fixed[0]),
        finish(dk, fixed[1]),
        finish(dv, fixed[2]),
        dgate,
        dbeta.T,
        conv_sum,
        decay_sum.reshape(channels),
    )


MAPS_GROUP = 8
GRADS_GROUP = 4


def solution(mesh):
    inner = Mesh(mesh.devices.reshape(4, 4, 8, 2), SEQ + ("head",))
    wide = P(SEQ, "head")
    in_specs = (wide, wide, wide, wide, wide, P(None, None, "head"), P("head"), wide)
    out_specs = (wide, wide, wide, wide, wide, P(None, None, "head"), P("head"))
    return jax.shard_map(
        per_device, mesh=inner, in_specs=in_specs, out_specs=out_specs, check_vma=False
    )
```
